256 devices in a mesh: row: 32 (over x, y, core), col: 8 (over z).
Axes of the slice: x: 4, y: 4, z: 8, core: 2. Of those that a mesh axis runs over, the one named last changes fastest.
Arguments:
- trailing_in: float32 [2, 32, 256, 8, 8, 256], P(None, 'row', None, None, 'col'), may hold values from 0 to 4, as said below
Outputs:
- factored: float32 [2, 32, 256, 8, 8, 256], P(None, 'row', None, None, 'col')
The draws below stay inside these ranges and needn't reach their ends.
Inputs may be any that keep to these rules, and one draw needn't show every extreme that they name: `trailing_in`: the matrix is symmetric and positive definite.
All inputs are finite; a program needn't handle non-finite values.
Results may differ from the reference program's by a relative error of at most 0.0003.
Values sent between devices are 32-bit elements; how exact they have to be, the bound alone decides.
A program may use at most 64 MiB of HBM per device.

```python
import jax
import jax.numpy as jnp
from jax import lax

NB = 256
LR = 2
LC = 8
N_ROW = 32
N_COL = 8


def draw_trailing_in(key, part):
    key = jax.random.fold_in(key, 11)
    matrix_order = LR * N_ROW * NB
    key_points, key_noise = jax.random.split(key)
    located = jax.random.normal(key_points, (matrix_order, 8), jnp.float32)
    noise_var = jnp.exp(jax.random.uniform(key_noise, (matrix_order,), jnp.float32, jnp.log(0.3), jnp.log(3.0)))
    col_ids = jnp.arange(matrix_order, dtype=jnp.int32)

    def tile_rows(tile_index):
        start = tile_index * NB
        block = lax.dynamic_slice_in_dim(located, start, NB, 0)
        block_noise = lax.dynamic_slice_in_dim(noise_var, start, NB, 0)
        differ = block[:, None, :] - located[None, :, :]
        distance = jnp.sum(differ * differ, axis=-1)
        row_ids = start + jnp.arange(NB, dtype=jnp.int32)
        on_diagonal = row_ids[:, None] == col_ids[None, :]
        return jnp.exp(-0.25 * distance) + jnp.where(on_diagonal, block_noise[:, None], jnp.float32(0.0))
    whole = lax.map(tile_rows, jnp.arange(matrix_order // NB, dtype=jnp.int32))
    return whole.reshape(LR, N_ROW, NB, LC, N_COL, NB).astype(jnp.float32)


def setup_inputs(seed: int = 0) -> dict:
    splits = jax.random.split(jax.random.key(seed), 2)
    trailing_in = draw_trailing_in(jax.random.fold_in(splits[1], 71), 0)
    return {"trailing_in": trailing_in}


HIGHEST_PRECISION = lax.Precision.HIGHEST

def solve_panel(factor_diag, column):
    return jax.scipy.linalg.solve_triangular(factor_diag, column.T, lower=True).T

def reference(trailing_in):
    matrix_order = LR * N_ROW * NB
    kernel = trailing_in.reshape(matrix_order, matrix_order)
    tile_count = matrix_order // NB
    first_col = kernel[:, :NB]
    factor_zero = jnp.linalg.cholesky(first_col[:NB])
    panel_zero = solve_panel(factor_zero, first_col)
    panel_zero = panel_zero.at[:NB].set(factor_zero)
    second_col = kernel[:, NB:2 * NB] - jnp.dot(panel_zero.astype(jnp.float32), panel_zero[NB:2 * NB].T.astype(jnp.float32), precision=HIGHEST_PRECISION, preferred_element_type=jnp.float32)
    factor_one = jnp.linalg.cholesky(second_col[NB:2 * NB])
    panel_one = solve_panel(factor_one, second_col)
    panel_one = panel_one.at[:NB].set(jnp.float32(0.0)).at[NB:2 * NB].set(factor_one)
    panels = jnp.concatenate([panel_zero, panel_one], axis=1)
    col_tiles = jnp.arange(matrix_order, dtype=jnp.int32) // NB

    def final_rows(tile_index):
        start = tile_index * NB
        kernel_block = lax.dynamic_slice_in_dim(kernel, start, NB, 0)
        panel_block = lax.dynamic_slice_in_dim(panels, start, NB, 0)
        updated = kernel_block - jnp.dot(panel_block.astype(jnp.float32), panels.T.astype(jnp.float32), precision=HIGHEST_PRECISION, preferred_element_type=jnp.float32)
        values = jnp.concatenate([panel_block, updated[:, 2 * NB:]], axis=1)
        keep = col_tiles <= tile_index
        return jnp.where(keep[None, :], values, jnp.float32(0.0))
    result = lax.map(final_rows, jnp.arange(tile_count, dtype=jnp.int32))
    return result.reshape(LR, N_ROW, NB, LC, N_COL, NB)
```

```python
import jax
import jax.numpy as jnp
from jax import lax
from jax.experimental import pallas as pl
from jax.experimental.pallas import tpu as pltpu
from jax.sharding import PartitionSpec as P

NB = 256
H = 128
F32 = jnp.float32
BF = jnp.bfloat16
HI = lax.Precision.HIGHEST
MESH = pl.DeviceIdType.MESH
NT = (((1,), (1,)), ((), ()))
NN = (((1,), (0,)), ((), ()))
STAGE = (0, 4, 7, 9, 10)


def blk(i, k):
    return STAGE[k] + i - k


def lane_splat(x, j):
    return jnp.broadcast_to(x[:, j:j + 1], (8, H))


def row_splat(x, s):
    return jnp.broadcast_to(x[s:s + 1, :], (8, H))


def tree(xs):
    xs = list(xs)
    while len(xs) > 1:
        xs = [xs[i] + xs[i + 1] if i + 1 < len(xs) else xs[i] for i in range(0, len(xs), 2)]
    return xs[0]


def strip(A, I):
    sub = lax.broadcasted_iota(jnp.int32, (8, H), 0)
    S, T = A[0], I[0]
    cols = [lane_splat(S, j) for j in range(8)]
    D = {(t, j): row_splat(cols[j], t) for j in range(8) for t in range(j, 8)}
    rec, rs, l = [], [], {}
    for s in range(8):
        p = D[s, s]
        r = 1.0 / p
        rec.append(r)
        rs.append(lax.rsqrt(p))
        for t in range(s + 1, 8):
            l[t, s] = D[t, s] * r
        for j in range(s + 1, 8):
            for t in range(j, 8):
                D[t, j] = D[t, j] - l[t, s] * D[j, s]
    u = {}
    for j in range(8):
        for t in range(j + 1, 8):
            acc = -l[t, j]
            for m in range(j + 1, t):
                acc = acc - l[t, m] * u[m, j]
            u[t, j] = acc
    ur = {(t, j): (rec[t] if t == j else u[t, j] * rec[t]) for j in range(8) for t in range(j, 8)}
    dinv = {}
    for i in range(8):
        for j in range(i + 1):
            dinv[i, j] = tree([ur[t, i] if t == j else ur[t, i] * u[t, j] for t in range(i, 8)])
    b0, b1, b2 = (sub & 1) == 1, (sub & 2) == 2, (sub & 4) == 4

    def assemble(v):
        a = [jnp.where(b0, v[2 * i + 1], v[2 * i]) for i in range(4)]
        b = [jnp.where(b1, a[2 * i + 1], a[2 * i]) for i in range(2)]
        return jnp.where(b2, b[1], b[0])

    zero = jnp.zeros((8, H), F32)
    one = jnp.ones((8, H), F32)
    srow = [row_splat(S, s) for s in range(8)]
    trow = [row_splat(T, s) for s in range(8)]
    dcol = [assemble([dinv[max(t, s), min(t, s)] for t in range(8)]) for s in range(8)]
    Z = tree([dcol[s] * srow[s] for s in range(8)])
    ZT = tree([dcol[s] * trow[s] for s in range(8)])
    ucol = [assemble([zero if t < s else (one if t == s else u[t, s]) for t in range(8)]) for s in range(8)]
    out = assemble(rs) * tree([ucol[s] * trow[s] for s in range(8)])
    zrow = [row_splat(Z, s) for s in range(8)]
    ztrow = [row_splat(ZT, s) for s in range(8)]
    An, In = [], []
    for g in range(1, len(A)):
        a = [lane_splat(A[g], s) for s in range(8)]
        An.append(pltpu.roll(A[g] - tree([a[s] * zrow[s] for s in range(8)]), H - 8, 1))
        In.append(I[g] - tree([a[s] * ztrow[s] for s in range(8)]))
    An.append(zero)
    In.append(zero)
    return An, In, out


def chol_inv(a, out_ref):
    sub = lax.broadcasted_iota(jnp.int32, (8, H), 0)
    lane = lax.broadcasted_iota(jnp.int32, (8, H), 1)
    A = [a[8 * g:8 * g + 8, :] for g in range(16)]
    I = [jnp.where(lane == sub + 8 * g, 1.0, 0.0).astype(F32) for g in range(16)]

    def body(k, c):
        An, In, out = strip(list(c[:16]), list(c[16:]))
        out_ref[pl.ds(pl.multiple_of(8 * k, 8), 8), :] = out
        return tuple(An) + tuple(In)

    lax.fori_loop(0, 16, body, tuple(A) + tuple(I))


def split(a):
    h = a.astype(BF)
    return h, (a - h.astype(F32)).astype(BF)


def dot3(a, b, dims):
    def g(p, q):
        return lax.dot_general(p, q, dims, preferred_element_type=F32)
    return g(a[0], b[0]) + (g(a[0], b[1]) + g(a[1], b[0]))


def dot_hi(a, b):
    return lax.dot_general(a, b, NT, precision=HI, preferred_element_type=F32)


def kernel(x, o, tiles, cols, rows, corner, fac, cm, prow, phi, plo, cthi, ctlo,
           ld, ldc, ldr, st, colsem, rowsem, csem, fsem, s1, s2, s3, s4, sr, sc, fz, fx, fy, fk):
    r = lax.axis_index("row")
    z = lax.axis_index("col")
    px, py, k = r // 8, (r // 2) % 4, r % 2
    u = jnp.where(k == 0, px, py)
    v = jnp.where(k == 0, py, px)

    def plane(uu, vv):
        xx = jnp.where(k == 0, uu, vv)
        yy = jnp.where(k == 0, vv, uu)
        return (xx * 8 + yy * 2 + k, z)

    partner = (r + 1 - 2 * k, z)
    root = (r == 0) & (z == 0)

    def load(a, b, h):
        return pltpu.make_async_copy(x.at[a, :, b, h, :], tiles.at[a, b, :, pl.ds(h * H, H)], ld.at[a, b, h])

    def load_col(b, h):
        return pltpu.make_async_copy(x.at[0, :, b, h, :], cols.at[k, b, :, pl.ds(h * H, H)], ldc.at[b, h])

    def load_row(a, h):
        return pltpu.make_async_copy(x.at[a, :, 0, h, :], rows.at[z, a, :, pl.ds(h * H, H)], ldr.at[a, h])

    @pl.when(z < 2)
    def _():
        for a in range(2):
            for h in range(2):
                load_row(a, h).start()

    @pl.when(r < 2)
    def _():
        for b in (2, 3, 4, 5, 6, 7, 0, 1):
            for h in range(2):
                load_col(b, h).start()

    for a in range(2):
        for b in range(8):
            for h in range(2):
                load(a, b, h).start()

    barrier = pltpu.get_barrier_semaphore()

    def greet(dev):
        pl.semaphore_signal(barrier, inc=1, device_id=dev, device_id_type=MESH)

    for d in range(1, 4):
        greet((((px + d) % 4) * 8 + py * 2 + k, z))
        greet((px * 8 + ((py + d) % 4) * 2 + k, z))
    greet(partner)
    for d in range(1, 8):
        greet((r, (z + d) % 8))

    extra = (r == 1) & (z == 1)

    @pl.when(extra)
    def _():
        greet((0, 0))

    @pl.when(root)
    def _():
        greet((1, 1))

    pl.semaphore_wait(barrier, jnp.where(root | extra, 15, 14))

    def send(src, dst, ss, rs, dev):
        return pltpu.make_async_remote_copy(src_ref=src, dst_ref=dst, send_sem=ss, recv_sem=rs, device_id=dev, device_id_type=MESH)

    def corner_send(i, dev):
        return send(rows.at[i, 0], corner.at[i], sc.at[0], csem.at[i], dev)

    def row_send(p, a, n, ds):
        zz = (z + (8 - ds if p == 0 else ds)) % 8
        return send(rows.at[p, a], rows.at[p, a], sr.at[p, n, a], rowsem.at[p, a], (r, zz))

    pos = [(8 - z) % 8, (z + 7) % 8]
    hops = {0: (3, 1, 7), 3: (2, 1, 7), 5: (1,)}

    def row_wait(p, a):
        send(rows.at[p, a], rows.at[p, a], sr.at[p, 0, a], rowsem.at[p, a], (r, z)).wait_recv()

    def col_send(q, n, e, b, dev):
        return send(cols.at[k, b], cols.at[k, b], q.at[n, e], colsem.at[k, b], dev)

    def col_wait(kk, b):
        send(cols.at[kk, b], cols.at[kk, b], s4.at[b], colsem.at[kk, b], partner).wait_recv()

    def give(b):
        return send(cols.at[k, b], cols.at[k, b], s4.at[b], colsem.at[k, b], partner)

    def level1(n, e):
        vv = (2, 1, 3)[n]
        return col_send(s1, n, e, 2 * vv + e, plane(0, vv))

    def level2(n, e):
        return col_send(s2, n, e, 2 * v + e, plane((2, 1, 3)[n], v))

    def level3(n, e):
        return col_send(s3, n, e, 2 * v + e, plane(u, (v + (2, 1, 3)[n]) % 4))

    def back(n):
        return (u == 0) & ((v + (2, 1, 3)[n]) % 4 == 0)

    src = r < 2

    @pl.when(z < 2)
    def _():
        for a in range(2):
            for h in range(2):
                load_row(a, h).wait()

    @pl.when((r == 1) & (z == 0))
    def _():
        corner_send(0, (0, 0)).start()

    @pl.when(extra)
    def _():
        corner_send(1, (0, 0)).start()

    for p in range(2):
        @pl.when(z == p)
        def _():
            for n in range(3):
                for a in range(2):
                    row_send(p, a, n, hops[0][n]).start()

    @pl.when(src)
    def _():
        for b in (2, 3, 4, 5, 6, 7, 0, 1):
            for h in range(2):
                load_col(b, h).wait()
        for e in range(2):
            for n in range(3):
                level1(n, e).start()
        for e in range(2):
            for n in range(3):
                level2(n, e).start()
        for e in range(2):
            for n in range(3):
                @pl.when(jnp.logical_not(back(n)))
                def _():
                    level3(n, e).start()
        for b in range(8):
            give(b).start()

    @pl.when((u == 0) & (v > 0))
    def _():
        for e in range(2):
            col_wait(k, 2 * v + e)
            for n in range(3):
                level2(n, e).start()
            for n in range(3):
                @pl.when(jnp.logical_not(back(n)))
                def _():
                    level3(n, e).start()
            give(2 * v + e).start()

    def row_forward(at):
        for p in range(2):
            @pl.when(pos[p] == at)
            def _():
                for a in range(2):
                    row_wait(p, a)
                    for n in range(len(hops[at])):
                        row_send(p, a, n, hops[at][n]).start()

    def stage_ref(s):
        return fac.at[pl.ds(STAGE[s], STAGE[s + 1] - STAGE[s])]

    def fac_send(s, ss, dev):
        return send(stage_ref(s), stage_ref(s), ss, fsem.at[s], dev)

    @pl.when(root)
    def _():
        for i in range(2):
            for j in range(i + 1):
                cm[i, j] = rows[0, 0, i * H:(i + 1) * H, j * H:(j + 1) * H]
        for s in range(4):
            chol_inv(cm[s, s], fac.at[blk(s, s)])
            if s == 0:
                send(rows.at[0, 0], corner.at[0], sc.at[0], csem.at[0], (r, z)).wait_recv()
                for i in range(2):
                    for j in range(2):
                        cm[2 + i, j] = corner[0, i * H:(i + 1) * H, j * H:(j + 1) * H]
                send(rows.at[0, 0], corner.at[1], sc.at[0], csem.at[1], (r, z)).wait_recv()
                for i in range(2):
                    for j in range(i + 1):
                        cm[2 + i, 2 + j] = corner[1, i * H:(i + 1) * H, j * H:(j + 1) * H]
            for i in range(s + 1, 4):
                fac[blk(i, s)] = dot_hi(cm[i, s], fac[blk(s, s)])
            for d in (4, 3, 5, 2, 6, 1, 7):
                fac_send(s, fz.at[s, d - 1], (0, d)).start()
            for n in range(3):
                fac_send(s, fx.at[s, n], ((2, 1, 3)[n] * 8, z)).start()
            for n in range(3):
                fac_send(s, fy.at[s, n], ((2, 1, 3)[n] * 2, z)).start()
            fac_send(s, fk.at[s], partner).start()
            for i in range(s + 1, 4):
                for j in range(s + 1, i + 1):
                    cm[i, j] = cm[i, j] - dot_hi(fac[blk(i, s)], fac[blk(j, s)])

    row_forward(3)

    @pl.when(u > 0)
    def _():
        for e in range(2):
            col_wait(k, 2 * v + e)
            for n in range(3):
                level3(n, e).start()
            give(2 * v + e).start()

    row_forward(5)

    @pl.when(jnp.logical_not(src))
    def _():
        for n in (1, 2, 0):
            for e in range(2):
                b = 2 * ((v + (2, 1, 3)[n]) % 4) + e
                col_wait(k, b)
                give(b).start()

    def store(a, b, h):
        return pltpu.make_async_copy(tiles.at[a, b, :, pl.ds(h * H, H)], o.at[a, :, b, h, :], st.at[a, b, h])

    def wait_loads(t, c):
        for h in range(2):
            load(t // 8, t % 8, h).wait()

        @pl.when(r + 32 * (t // 8) < z + 8 * (t % 8))
        def _():
            tiles[t // 8, t % 8] = jnp.zeros((NB, NB), F32)
            for h in range(2):
                store(t // 8, t % 8, h).start()
        return c

    lax.fori_loop(0, 16, wait_loads, 0)

    def fac_arrive(s):
        @pl.when(jnp.logical_not(root))
        def _():
            fac_send(s, fk.at[s], partner).wait_recv()

            @pl.when((px == 0) & (py == 0) & (k == 0))
            def _():
                for n in range(3):
                    fac_send(s, fx.at[s, n], ((2, 1, 3)[n] * 8, z)).start()

            @pl.when((py == 0) & (k == 0))
            def _():
                for n in range(3):
                    fac_send(s, fy.at[s, n], (px * 8 + (2, 1, 3)[n] * 2, z)).start()

            @pl.when(k == 0)
            def _():
                fac_send(s, fk.at[s], partner).start()

    def solve(s):
        w = (s % 2) * H
        fs = {m: split(fac[blk(s, m)]) for m in range(s + 1)}
        at = slice(s * H, (s + 1) * H)
        for a in range(2):
            t = rows[s // 2, a, :, w:w + H]
            for m in range(s):
                ms = slice(m * H, (m + 1) * H)
                t = t - dot3((phi[a, :, ms], plo[a, :, ms]), fs[m], NT)
            t = dot3(split(t), fs[s], NT)
            prow[a, :, at] = t
            phi[a, :, at], plo[a, :, at] = split(t)

        def col(b, c):
            @pl.when(z + 8 * b <= r + 32)
            def _():
                t = cols[s // 2, b, w:w + H, :]
                for m in range(s):
                    ms = slice(m * H, (m + 1) * H)
                    t = t - dot3(fs[m], (cthi[b, ms, :], ctlo[b, ms, :]), NN)
                t = dot3(fs[s], split(t), NN)
                cthi[b, at, :], ctlo[b, at, :] = split(t)
            return c

        lax.fori_loop(0, 8, col, 0)

    def update(p, last):
        at = slice(p * NB, (p + 1) * NB)

        def tile(t, c):
            a, b = t // 8, t % 8

            @pl.when((r + 32 * a >= z + 8 * b) & (z + 8 * b >= 2))
            def _():
                d = dot3((phi[a, :, at], plo[a, :, at]), (cthi[b, at, :], ctlo[b, at, :]), NN)
                tiles[a, b] = tiles[a, b] - d
                if last:
                    for h in range(2):
                        store(a, b, h).start()
            return c

        lax.fori_loop(0, 16, tile, 0)

    for s in range(4):
        fac_arrive(s)
        if s % 2 == 0:
            p = s // 2
            for a in range(2):
                if p == 0:
                    @pl.when((z != 0) & (pos[0] != 3) & (pos[0] != 5))
                    def _():
                        row_wait(0, a)
                else:
                    @pl.when((z != 1) & (pos[1] != 3) & (pos[1] != 5))
                    def _():
                        row_wait(1, a)

            @pl.when(k != p)
            def _():
                for b in range(8):
                    col_wait(p, b)
        solve(s)
        if s == 1:
            update(0, False)

    for p in range(2):
        @pl.when(z == p)
        def _():
            for a in range(2):
                @pl.when((r + 32 * a >= p))
                def _():
                    t = prow[a, :, p * NB:(p + 1) * NB]
                    ri = lax.broadcasted_iota(jnp.int32, (NB, NB), 0)
                    ci = lax.broadcasted_iota(jnp.int32, (NB, NB), 1)
                    keep = (ri >= ci) | (r + 32 * a > p)
                    tiles[a, 0] = jnp.where(keep, t, 0.0)
                    for h in range(2):
                        store(a, 0, h).start()

    update(1, True)

    @pl.when((r == 1) & (z == 0))
    def _():
        corner_send(0, (0, 0)).wait_send()

    @pl.when(extra)
    def _():
        corner_send(1, (0, 0)).wait_send()

    for p in range(2):
        for at in (0, 3, 5):
            @pl.when(pos[p] == at)
            def _():
                for n in range(len(hops[at])):
                    for a in range(2):
                        row_send(p, a, n, hops[at][n]).wait_send()
    for e in range(2):
        for n in range(3):
            @pl.when(src)
            def _():
                level1(n, e).wait_send()

            @pl.when(u == 0)
            def _():
                level2(n, e).wait_send()

            @pl.when(jnp.logical_not(back(n)))
            def _():
                level3(n, e).wait_send()
    for b in range(8):
        give(b).wait_send()
    for s in range(4):
        @pl.when(root)
        def _():
            for d in range(1, 8):
                fac_send(s, fz.at[s, d - 1], (0, d)).wait_send()

        @pl.when((px == 0) & (py == 0) & (k == 0))
        def _():
            for n in range(3):
                fac_send(s, fx.at[s, n], ((2, 1, 3)[n] * 8, z)).wait_send()

        @pl.when((py == 0) & (k == 0))
        def _():
            for n in range(3):
                fac_send(s, fy.at[s, n], (px * 8 + (2, 1, 3)[n] * 2, z)).wait_send()

        @pl.when(k == 0)
        def _():
            fac_send(s, fk.at[s], partner).wait_send()

    def drain(t, c):
        for h in range(2):
            store(t // 8, t % 8, h).wait()
        return c

    lax.fori_loop(0, 16, drain, 0)


def on_device(trailing_in):
    x = trailing_in.reshape(2, NB, 8, 2, H)
    dma = pltpu.SemaphoreType.DMA
    out = pl.pallas_call(
        kernel,
        out_shape=jax.ShapeDtypeStruct(x.shape, F32),
        in_specs=[pl.BlockSpec(memory_space=pl.ANY)],
        out_specs=pl.BlockSpec(memory_space=pl.ANY),
        scratch_shapes=[
            pltpu.VMEM((2, 8, NB, NB), F32),
            pltpu.VMEM((2, 8, NB, NB), F32),
            pltpu.VMEM((2, 2, NB, NB), F32),
            pltpu.VMEM((2, NB, NB), F32),
            pltpu.VMEM((10, H, H), F32),
            pltpu.VMEM((4, 4, H, H), F32),
            pltpu.VMEM((2, NB, 2 * NB), F32),
            pltpu.VMEM((2, NB, 2 * NB), BF),
            pltpu.VMEM((2, NB, 2 * NB), BF),
            pltpu.VMEM((8, 2 * NB, NB), BF),
            pltpu.VMEM((8, 2 * NB, NB), BF),
            dma((2, 8, 2)), dma((8, 2)), dma((2, 2)), dma((2, 8, 2)),
            dma((2, 8)), dma((2, 2)), dma((2,)), dma((4,)),
            dma((3, 2)), dma((3, 2)), dma((3, 2)), dma((8,)),
            dma((2, 3, 2)), dma((1,)), dma((4, 7)), dma((4, 3)), dma((4, 3)), dma((4,)),
        ],
        compiler_params=pltpu.CompilerParams(
            collective_id=0, has_side_effects=True, vmem_limit_bytes=56 << 20
        ),
    )(x)
    return out.reshape(trailing_in.shape)


def solution(mesh):
    spec = P(None, "row", None, None, "col", None)
    return jax.shard_map(on_device, mesh=mesh, in_specs=(spec,), out_specs=spec, check_vma=False)
```

```python
import jax
import jax.numpy as jnp
from jax import lax
from jax.experimental import pallas as pl
from jax.experimental.pallas import tpu as pltpu
from jax.sharding import PartitionSpec as P

NB = 256
H = 128
F32 = jnp.float32
BF = jnp.bfloat16
HI = lax.Precision.HIGHEST
MESH = pl.DeviceIdType.MESH
NT = (((1,), (1,)), ((), ()))
NN = (((1,), (0,)), ((), ()))
STAGE = (0, 4, 7, 9, 10)


def blk(i, k):
    return STAGE[k] + i - k


def lane_splat(x, j):
    return jnp.broadcast_to(x[:, j:j + 1], (8, H))


def row_splat(x, s):
    return jnp.broadcast_to(x[s:s + 1, :], (8, H))


def tree(xs):
    xs = list(xs)
    while len(xs) > 1:
        xs = [xs[i] + xs[i + 1] if i + 1 < len(xs) else xs[i] for i in range(0, len(xs), 2)]
    return xs[0]


def assemble(v, sub):
    b0, b1, b2 = (sub & 1) == 1, (sub & 2) == 2, (sub & 4) == 4
    a = [v[2 * i] if v[2*i] is v[2*i+1] else jnp.where(b0, v[2 * i + 1], v[2 * i]) for i in range(4)]
    b = [a[2 * i] if a[2*i] is a[2*i+1] else jnp.where(b1, a[2 * i + 1], a[2 * i]) for i in range(2)]
    return b[0] if b[0] is b[1] else jnp.where(b2, b[1], b[0])


def chol_inv(a, out_ref, n=16):
    sub = lax.broadcasted_iota(jnp.int32, (8, H), 0)
    lane = lax.broadcasted_iota(jnp.int32, (8, H), 1)
    zero = jnp.zeros((8, H), F32)
    one = jnp.ones((8, H), F32)
    A = [a[8 * g:8 * g + 8, :] for g in range(n)]
    I = [jnp.where(lane == sub + 8 * g, 1.0, 0.0).astype(F32) for g in range(n)]
    c = [lane_splat(A[0], j) for j in range(8)]
    for k in range(n):
        w = 8 * k
        more = k + 1 < n
        if more:
            a1 = [lane_splat(A[k + 1], w + s) for s in range(8)]
            cn = [lane_splat(A[k + 1], w + 8 + j) for j in range(8)]
        D = {(t, j): row_splat(c[j], t) for j in range(8) for t in range(j, 8)}
        rec, rs, l = [], [], {}
        for s in range(8):
            p = D[s, s]
            r = 1.0 / p
            rec.append(r)
            rs.append(lax.rsqrt(p))
            for t in range(s + 1, 8):
                l[t, s] = D[t, s] * r
            for j in range(s + 1, 8):
                for t in range(j, 8):
                    D[t, j] = D[t, j] - l[t, s] * D[j, s]
            if more:
                x = a1[s]
                m = x * r
                for j in range(8):
                    cn[j] = cn[j] - m * row_splat(x, j)
                for t in range(s + 1, 8):
                    a1[t] = a1[t] - x * l[t, s]
        u = {}
        for j in range(8):
            for t in range(j + 1, 8):
                u[t, j] = -tree([l[t, j]] + [l[t, m] * u[m, j] for m in range(j + 1, t)])
        S, T = A[k], I[k]
        ucol = [assemble([zero if t < s else (one if t == s else u[t, s]) for t in range(8)], sub) for s in range(8)]
        T1 = tree([ucol[s] * row_splat(T, s) for s in range(8)])
        out_ref[w:w + 8, :] = assemble(rs, sub) * T1
        if more:
            recv = assemble(rec, sub)
            S1 = tree([ucol[s] * row_splat(S, s) for s in range(8)]) * recv
            T2 = T1 * recv
            vcol = [assemble([u[t, s] if s < t else (one if s == t else zero) for s in range(8)], sub) for t in range(8)]
            Z = tree([vcol[t] * row_splat(S1, t) for t in range(8)])
            ZT = tree([vcol[t] * row_splat(T2, t) for t in range(8)])
            zrow = [row_splat(Z, s) for s in range(8)]
            ztrow = [row_splat(ZT, s) for s in range(8)]
            for g in range(k + 1, n):
                ag = [lane_splat(A[g], w + s) for s in range(8)]
                A[g] = A[g] - tree([ag[s] * zrow[s] for s in range(8)])
                I[g] = I[g] - tree([ag[s] * ztrow[s] for s in range(8)])
            c = cn


def split(a):
    h = a.astype(BF)
    return h, (a - h.astype(F32)).astype(BF)


def dot3(a, b, dims):
    def g(p, q):
        return lax.dot_general(p, q, dims, preferred_element_type=F32)
    return g(a[0], b[0]) + (g(a[0], b[1]) + g(a[1], b[0]))


def dot_hi(a, b):
    return lax.dot_general(a, b, NT, precision=HI, preferred_element_type=F32)


CH = 64
NC = 2 * NB // CH
PER = NB // CH
HOP = 4
DIRS = ((1, 0), (0, 1), (-1, 0), (0, -1))
PARENT = {(1, 0): 0, (2, 0): 0, (1, 1): 1, (1, 3): 3, (2, 1): 0, (1, 2): 1, (0, 1): 2, (0, 3): 2,
          (3, 0): 0, (2, 3): 3, (2, 2): 0, (0, 2): 2, (3, 1): 0, (3, 3): 0, (3, 2): 0}
FSTEP = (7, 10, 13, 16)
FLEVEL = 3
STEPS = NC + 5 * HOP
OTHER = (2, 1, 3)
ZFAN = {0: (2, 6, 1, 7), 2: (4, 3), 6: (5,)}


def tree_tables():
    depth = {(0, 0): 0}
    kids = {v: [] for v in list(PARENT) + [(0, 0)]}
    for v, d in PARENT.items():
        kids[(v[0] - DIRS[d][0]) % 4, (v[1] - DIRS[d][1]) % 4].append(d)
    while len(depth) < 16:
        for v, d in PARENT.items():
            up = ((v[0] - DIRS[d][0]) % 4, (v[1] - DIRS[d][1]) % 4)
            if up in depth:
                depth[v] = depth[up] + 1
    child = [sum(1 << (4 * v[0] + v[1]) for v in kids if d in kids[v]) for d in range(4)]
    bits = [sum(1 << (4 * v[0] + v[1]) for v in depth if depth[v] >> n & 1) for n in range(3)]
    return child, bits


CHILD, DEPTH = tree_tables()


def bit(mask, n):
    hit = False
    for i in range(16):
        if mask >> i & 1:
            hit = (n == i) | hit
    return hit


def kernel(x, tiles, cols, rows, corner, fac, cm, linv, phi, plo, cthi, ctlo,
           ld, ldc, ldr, colsem, givesem, rowsem, csem, fsem, scol, sgive, srow, sc, fz, fx, fy, fk):
    r = lax.axis_index("row")
    z = lax.axis_index("col")
    px, py, k = r // 8, (r // 2) % 4, r % 2
    partner = (r + 1 - 2 * k, z)
    root = (r == 0) & (z == 0)
    src = r < 2
    extra = (r == 1) & (z == 1)

    def load(a, b, h):
        return pltpu.make_async_copy(x.at[a, :, b, h, :], tiles.at[a, b, :, pl.ds(h * H, H)], ld.at[a, b, h])

    def load_col(b, h):
        return pltpu.make_async_copy(x.at[0, :, b, h, :], cols.at[k, b, :, pl.ds(h * H, H)], ldc.at[b, h])

    def load_row(a, h):
        return pltpu.make_async_copy(x.at[a, :, 0, h, :], rows.at[z, a, :, pl.ds(h * H, H)], ldr.at[a, h])

    @pl.when(z < 2)
    def _():
        for a in range(2):
            for h in range(2):
                load_row(a, h).start()

    @pl.when(src)
    def _():
        for b in range(8):
            for h in range(2):
                load_col(b, h).start()

    for a in range(2):
        for b in range(8):
            for h in range(2):
                load(a, b, h).start()

    barrier = pltpu.get_barrier_semaphore()

    def greet(dev):
        pl.semaphore_signal(barrier, inc=1, device_id=dev, device_id_type=MESH)

    for d in (1, 3):
        greet((((px + d) % 4) * 8 + py * 2 + k, z))
        greet((px * 8 + ((py + d) % 4) * 2 + k, z))
    greet(partner)
    for d in (1, 7):
        greet((r, (z + d) % 8))

    @pl.when(k == 0)
    def _():
        greet((((px + 2) % 4) * 8 + py * 2, z))
        greet((px * 8 + ((py + 2) % 4) * 2, z))

    @pl.when(r == 0)
    def _():
        for d in (2, 6):
            greet((0, (z + d) % 8))

    @pl.when(extra)
    def _():
        greet((0, 0))

    @pl.when(root)
    def _():
        greet((1, 1))

    @pl.when(z < 2)
    def _():
        for a in range(2):
            for h in range(2):
                load_row(a, h).wait()

    @pl.when(root)
    def _():
        for i in range(2):
            for j in range(i + 1):
                cm[i, j] = rows[0, 0, i * H:(i + 1) * H, j * H:(j + 1) * H]
        chol_inv(cm[0, 0], linv)

    peers = 7 + jnp.where(k == 0, 2, 0) + jnp.where(r == 0, 2, 0) + jnp.where(root | extra, 1, 0)
    pl.semaphore_wait(barrier, peers)

    def send(ref, ss, rs, dev, to=None):
        return pltpu.make_async_remote_copy(
            src_ref=ref, dst_ref=ref if to is None else to, send_sem=ss, recv_sem=rs, device_id=dev, device_id_type=MESH)

    def start(c):
        c.start()

    def wait_send(c):
        c.wait_send()

    def corner_send(i, dev):
        return send(rows.at[i, 0], sc.at[0], csem.at[i], dev, corner.at[i])

    def row_send(p, i, d, zz):
        ref = rows.at[p, i // PER, pl.ds((i % PER) * CH, CH)]
        return send(ref, srow.at[p, d, i], rowsem.at[p, i], (r, zz))

    row_depth = (jnp.where(z < 3, z, 8 - z),
                 jnp.where(z == 0, 1, jnp.where((z == 7) & (r > 0), 2, z - 1)))
    row_down = ((z == 0) | (z > 3), (z == 1) | ((z == 0) & (r > 0)))
    row_up = (z < 2, (z > 0) & ((z < 6) | ((z == 6) & (r == 0))))
    row_from = (z > 0, z != 1)
    row_first = (jnp.where(r == 0, PER, 0), jnp.where(r < 2, PER, 0))

    def row_spread(p, i, act):
        @pl.when(row_down[p])
        def _():
            act(row_send(p, i, 0, (z + 7) % 8))

        @pl.when(row_up[p])
        def _():
            act(row_send(p, i, 1, (z + 1) % 8))

    def row_step(p, step):
        i = step - row_depth[p] * HOP

        @pl.when((i >= row_first[p]) & (i < NC) & (row_down[p] | row_up[p]))
        def _():
            @pl.when(row_from[p])
            def _():
                row_send(p, i, 0, z).wait_recv()
            row_spread(p, i, start)

    frames, links = [], []
    fx_, fy_ = px, py
    for t in range(4):
        n = fx_ * 4 + fy_
        frames.append((bit(DEPTH[0], n).astype(jnp.int32) + 2 * bit(DEPTH[1], n).astype(jnp.int32)
                       + 4 * bit(DEPTH[2], n).astype(jnp.int32)) * HOP)
        links.append([bit(CHILD[d], n) for d in range(4)])
        fx_, fy_ = fy_, (4 - fx_) % 4

    def col_send(t, i, d, dev):
        ref = cols.at[k, t + 4 * (i // PER), pl.ds((i % PER) * CH, CH)]
        return send(ref, scol.at[t, d, i], colsem.at[t, i], dev)

    def col_spread(t, i, act):
        for d in range(4):
            dx, dy = DIRS[(d + t) % 4]

            @pl.when(links[t][d])
            def _():
                act(col_send(t, i, d, (((px + dx + 4) % 4) * 8 + ((py + dy + 4) % 4) * 2 + k, z)))

    def give(b):
        return send(cols.at[k, b], sgive.at[b], givesem.at[b], partner)

    def col_step(t, step):
        i = step - frames[t]

        @pl.when((i >= 0) & (i < NC))
        def _():
            @pl.when(jnp.logical_not(src))
            def _():
                col_send(t, i, 0, partner).wait_recv()
            col_spread(t, i, start)

            @pl.when(i % PER == PER - 1)
            def _():
                give(t + 4 * (i // PER)).start()

    def use(b):
        return px >= b - 4

    def fac_send(s, ss, dev):
        ref = fac.at[pl.ds(STAGE[s], STAGE[s + 1] - STAGE[s])]
        return send(ref, ss, fsem.at[s], dev)

    def fac_spread(s, act):
        for at, to in ZFAN.items():
            @pl.when((r == 0) & (z == at))
            def _():
                for d in to:
                    act(fac_send(s, fz.at[s, d - 1], (0, d)))

        @pl.when(r == 0)
        def _():
            for n in range(3):
                act(fac_send(s, fx.at[s, n], (OTHER[n] * 8, z)))

        @pl.when((py == 0) & (k == 0))
        def _():
            for n in range(3):
                act(fac_send(s, fy.at[s, n], (px * 8 + OTHER[n] * 2, z)))

        @pl.when(k == 0)
        def _():
            act(fac_send(s, fk.at[s], partner))

    def fac_wait(s):
        fac_send(s, fk.at[s], partner).wait_recv()

    relay = (k == 0) & (py == 0) & jnp.logical_not(root)
    level = (jnp.where((z > 2) & (z < 6), 1, 0) + jnp.where(px > 0, 1, 0)) * FLEVEL

    @pl.when((r == 1) & (z == 0))
    def _():
        corner_send(0, (0, 0)).start()

    @pl.when(extra)
    def _():
        corner_send(1, (0, 0)).start()

    @pl.when(src)
    def _():
        for b in range(8):
            for h in range(2):
                load_col(b, h).wait()

    def step_body(step, c):
        for p in range(2):
            row_step(p, step)
        for t in range(4):
            col_step(t, step)
        for s in range(4):
            @pl.when(relay & (step == FSTEP[s] + level))
            def _():
                fac_wait(s)
                fac_spread(s, start)
        return c

    lax.fori_loop(0, jnp.where(root, NC, jnp.where((r == 0) & (z > 5), STEPS + HOP, STEPS)), step_body, 0)

    @pl.when(root)
    def _():
        for i in range(2):
            send(rows.at[0, 0], sc.at[0], csem.at[i], partner, corner.at[i]).wait_recv()
        for i in range(2):
            for j in range(2):
                cm[2 + i, j] = corner[0, i * H:(i + 1) * H, j * H:(j + 1) * H]
            for j in range(i + 1):
                cm[2 + i, 2 + j] = corner[1, i * H:(i + 1) * H, j * H:(j + 1) * H]

        def stage(t, c):
            @pl.when(t > 0)
            def _():
                chol_inv(cm[t, t], linv)
            for s in range(4):
                @pl.when(t == s)
                def _():
                    fac[blk(s, s)] = linv[...]
                    for i in range(s + 1, 4):
                        fac[blk(i, s)] = dot_hi(cm[i, s], linv[...])
                    fac_spread(s, start)
                    for i in range(s + 1, 4):
                        for j in range(s + 1, i + 1):
                            cm[i, j] = cm[i, j] - dot_hi(fac[blk(i, s)], fac[blk(j, s)])
            return c

        lax.fori_loop(0, 4, stage, 0)

    for p in range(2):
        @pl.when(row_from[p] & jnp.logical_not(row_down[p] | row_up[p]))
        def _():
            def body(i, c):
                row_send(p, i, 0, z).wait_recv()
                return c
            lax.fori_loop(row_first[p], NC, body, 0)

    for b in range(8):
        give(b).wait_recv()

    for a in range(2):
        for b in range(8):
            for h in range(2):
                load(a, b, h).wait()

    def solve(s):
        w = (s % 2) * H
        at = slice(s * H, (s + 1) * H)
        done = slice(0, s * H)
        fs = split(fac[blk(s, s)])
        if s:
            fl = split(jnp.concatenate([fac[blk(s, m)] for m in range(s)], axis=1))
        for a in range(2):
            t = rows[s // 2, a, :, w:w + H]
            if s:
                t = t - dot3((phi[a, :, done], plo[a, :, done]), fl, NT)
            t = dot3(split(t), fs, NT)
            phi[a, :, at], plo[a, :, at] = split(t)

            @pl.when((z == s // 2) & (r + 32 * a >= z))
            def _():
                if w == 0:
                    tiles[a, 0, :, H:] = jnp.zeros((NB, H), F32)
                tiles[a, 0, :, w:w + H] = t

        def col(b):
            t = cols[s // 2, b, w:w + H, :]
            if s:
                t = t - dot3(fl, (cthi[b, done, :], ctlo[b, done, :]), NN)
            t = dot3(fs, split(t), NN)
            cthi[b, at, :], ctlo[b, at, :] = split(t)

        for b in range(5):
            col(b)
        for b in range(5, 8):
            @pl.when(use(b))
            def _():
                col(b)

    def update(lo, hi):
        at = slice(lo * H, hi * H)

        def tile(a, b):
            d = dot3((phi[a, :, at], plo[a, :, at]), (cthi[b, at, :], ctlo[b, at, :]), NN)
            if b == 0:
                d = jnp.where(z < 2, 0.0, d)
            tiles[a, b] = tiles[a, b] - d

        for b in range(5):
            tile(1, b)
        tile(0, 0)
        for n in range(1, 4):
            @pl.when(px >= n)
            def _():
                tile(1, 4 + n)
                tile(0, n)

    for s in range(4):
        @pl.when(jnp.logical_not(relay | root))
        def _():
            fac_wait(s)
            fac_spread(s, start)
        solve(s)
        if s == 1:
            update(0, 2)
        if s > 1:
            update(s, s + 1)

    for a in range(2):
        for b in range(8):
            @pl.when(r + 32 * a < z + 8 * b)
            def _():
                tiles[a, b] = jnp.zeros((NB, NB), F32)

    for p in range(2):
        @pl.when((z == p) & (r == p))
        def _():
            ri = lax.broadcasted_iota(jnp.int32, (NB, NB), 0)
            ci = lax.broadcasted_iota(jnp.int32, (NB, NB), 1)
            tiles[0, 0] = jnp.where(ri >= ci, tiles[0, 0], 0.0)

    @pl.when((r == 1) & (z == 0))
    def _():
        corner_send(0, (0, 0)).wait_send()

    @pl.when(extra)
    def _():
        corner_send(1, (0, 0)).wait_send()

    def sent(i, c):
        for p in range(2):
            @pl.when(i >= row_first[p])
            def _():
                row_spread(p, i, wait_send)
        for t in range(4):
            col_spread(t, i, wait_send)
        return c

    for b in range(8):
        give(b).wait_send()

    lax.fori_loop(0, NC, sent, 0)
    for s in range(4):
        fac_spread(s, wait_send)


def writer(t, o, buf, isem, osem):
    def get(a, b):
        return pltpu.make_async_copy(t.at[a, b], buf.at[a, b], isem.at[a, b])

    def put(a, b, h):
        return pltpu.make_async_copy(buf.at[a, b, :, pl.ds(h * H, H)], o.at[a, :, b, h, :], osem.at[a, b, h])

    which = [(a, b) for a in range(2) for b in range(8)]
    for w in which:
        get(*w).start()
    for w in which:
        get(*w).wait()
        for h in range(2):
            put(*w, h).start()
    for w in which:
        for h in range(2):
            put(*w, h).wait()


def on_device(trailing_in):
    x = trailing_in.reshape(2, NB, 8, 2, H)
    dma = pltpu.SemaphoreType.DMA
    t = pl.pallas_call(
        kernel,
        out_shape=jax.ShapeDtypeStruct((2, 8, NB, NB), F32),
        in_specs=[pl.BlockSpec(memory_space=pl.ANY)],
        out_specs=pl.BlockSpec(memory_space=pltpu.VMEM),
        scratch_shapes=[
            pltpu.VMEM((2, 8, NB, NB), F32),
            pltpu.VMEM((2, 2, NB, NB), F32),
            pltpu.VMEM((2, NB, NB), F32),
            pltpu.VMEM((10, H, H), F32),
            pltpu.VMEM((4, 4, H, H), F32),
            pltpu.VMEM((H, H), F32),
            pltpu.VMEM((2, NB, 2 * NB), BF),
            pltpu.VMEM((2, NB, 2 * NB), BF),
            pltpu.VMEM((8, 2 * NB, NB), BF),
            pltpu.VMEM((8, 2 * NB, NB), BF),
            dma((2, 8, 2)), dma((8, 2)), dma((2, 2)),
            dma((4, NC)), dma((8,)), dma((2, NC)), dma((2,)), dma((4,)),
            dma((4, 4, NC)), dma((8,)), dma((2, 2, NC)), dma((1,)),
            dma((4, 7)), dma((4, 3)), dma((4, 3)), dma((4,)),
        ],
        compiler_params=pltpu.CompilerParams(
            collective_id=0, has_side_effects=True, vmem_limit_bytes=56 << 20
        ),
    )(x)
    out = pl.pallas_call(
        writer,
        out_shape=jax.ShapeDtypeStruct(x.shape, F32),
        in_specs=[pl.BlockSpec(memory_space=pl.ANY)],
        out_specs=pl.BlockSpec(memory_space=pl.ANY),
        scratch_shapes=[pltpu.VMEM((2, 8, NB, NB), F32), dma((2, 8)), dma((2, 8, 2))],
        compiler_params=pltpu.CompilerParams(vmem_limit_bytes=56 << 20),
    )(t)
    return out.reshape(trailing_in.shape)


def solution(mesh):
    spec = P(None, "row", None, None, "col", None)
    return jax.shard_map(on_device, mesh=mesh, in_specs=(spec,), out_specs=spec, check_vma=False)
```

```python
import jax
import jax.numpy as jnp
from jax import lax
from jax.experimental import pallas as pl
from jax.experimental.pallas import tpu as pltpu
from jax.sharding import PartitionSpec as P

NB = 256
H = 128
F32 = jnp.float32
BF = jnp.bfloat16
HI = lax.Precision.HIGHEST
MESH = pl.DeviceIdType.MESH
NT = (((1,), (1,)), ((), ()))
NN = (((1,), (0,)), ((), ()))
STAGE = (0, 4, 7, 9, 10)


def blk(i, k):
    return STAGE[k] + i - k


def lane_splat(x, j):
    return jnp.broadcast_to(x[:, j:j + 1], (8, H))


def row_splat(x, s):
    return jnp.broadcast_to(x[s:s + 1, :], (8, H))


def tree(xs):
    xs = list(xs)
    while len(xs) > 1:
        xs = [xs[i] + xs[i + 1] if i + 1 < len(xs) else xs[i] for i in range(0, len(xs), 2)]
    return xs[0]


def assemble(v, sub):
    b0, b1, b2 = (sub & 1) == 1, (sub & 2) == 2, (sub & 4) == 4
    a = [v[2 * i] if v[2*i] is v[2*i+1] else jnp.where(b0, v[2 * i + 1], v[2 * i]) for i in range(4)]
    b = [a[2 * i] if a[2*i] is a[2*i+1] else jnp.where(b1, a[2 * i + 1], a[2 * i]) for i in range(2)]
    return b[0] if b[0] is b[1] else jnp.where(b2, b[1], b[0])


def chol_inv(a, out_ref, n=16):
    sub = lax.broadcasted_iota(jnp.int32, (8, H), 0)
    lane = lax.broadcasted_iota(jnp.int32, (8, H), 1)
    zero = jnp.zeros((8, H), F32)
    one = jnp.ones((8, H), F32)
    A = [a[8 * g:8 * g + 8, :] for g in range(n)]
    I = [jnp.where(lane == sub + 8 * g, 1.0, 0.0).astype(F32) for g in range(n)]
    c = [lane_splat(A[0], j) for j in range(8)]
    for k in range(n):
        w = 8 * k
        more = k + 1 < n
        if more:
            a1 = [lane_splat(A[k + 1], w + s) for s in range(8)]
            cn = [lane_splat(A[k + 1], w + 8 + j) for j in range(8)]
        D = {(t, j): row_splat(c[j], t) for j in range(8) for t in range(j, 8)}
        rec, rs, l = [], [], {}
        for s in range(8):
            p = D[s, s]
            r = 1.0 / p
            rec.append(r)
            rs.append(lax.rsqrt(p))
            for t in range(s + 1, 8):
                l[t, s] = D[t, s] * r
            for j in range(s + 1, 8):
                for t in range(j, 8):
                    D[t, j] = D[t, j] - l[t, s] * D[j, s]
            if more:
                x = a1[s]
                m = x * r
                for j in range(8):
                    cn[j] = cn[j] - m * row_splat(x, j)
                for t in range(s + 1, 8):
                    a1[t] = a1[t] - x * l[t, s]
        u = {}
        for j in range(8):
            for t in range(j + 1, 8):
                u[t, j] = -tree([l[t, j]] + [l[t, m] * u[m, j] for m in range(j + 1, t)])
        S, T = A[k], I[k]
        ucol = [assemble([zero if t < s else (one if t == s else u[t, s]) for t in range(8)], sub) for s in range(8)]
        T1 = tree([ucol[s] * row_splat(T, s) for s in range(8)])
        out_ref[w:w + 8, :] = assemble(rs, sub) * T1
        if more:
            recv = assemble(rec, sub)
            S1 = tree([ucol[s] * row_splat(S, s) for s in range(8)]) * recv
            T2 = T1 * recv
            vcol = [assemble([u[t, s] if s < t else (one if s == t else zero) for s in range(8)], sub) for t in range(8)]
            Z = tree([vcol[t] * row_splat(S1, t) for t in range(8)])
            ZT = tree([vcol[t] * row_splat(T2, t) for t in range(8)])
            zrow = [row_splat(Z, s) for s in range(8)]
            ztrow = [row_splat(ZT, s) for s in range(8)]
            for g in range(k + 1, n):
                ag = [lane_splat(A[g], w + s) for s in range(8)]
                A[g] = A[g] - tree([ag[s] * zrow[s] for s in range(8)])
                I[g] = I[g] - tree([ag[s] * ztrow[s] for s in range(8)])
            c = cn


def split(a):
    h = a.astype(BF)
    return h, (a - h.astype(F32)).astype(BF)


def dot3(a, b, dims):
    def g(p, q):
        return lax.dot_general(p, q, dims, preferred_element_type=F32)
    return g(a[0], b[0]) + (g(a[0], b[1]) + g(a[1], b[0]))


def dot_hi(a, b):
    return lax.dot_general(a, b, NT, precision=HI, preferred_element_type=F32)


CH = 64
NC = 2 * NB // CH
PER = NB // CH
HOP = 3
DIRS = ((1, 0), (0, 1), (-1, 0), (0, -1))
PARENT = {(1, 0): 0, (2, 0): 0, (1, 1): 1, (1, 3): 3, (2, 1): 0, (1, 2): 1, (0, 1): 2, (0, 3): 2,
          (3, 0): 0, (2, 3): 3, (2, 2): 0, (0, 2): 2, (3, 1): 0, (3, 3): 0, (3, 2): 0}
QUARTERED = 0
QSTEP = (0, 0)
ZSTEP = (8, 10, 13, 16)
FAR = 3
STEPS = max(QSTEP[1] + 4 * HOP + 1, NC + 5 * HOP, ZSTEP[3] + 2 * FAR + 1)
OTHER = (2, 1, 3)
ZFAN = {0: (2, 6), 2: (4, 3, 1), 6: (5, 7)}


def tree_tables():
    depth = {(0, 0): 0}
    kids = {v: [] for v in list(PARENT) + [(0, 0)]}
    for v, d in PARENT.items():
        kids[(v[0] - DIRS[d][0]) % 4, (v[1] - DIRS[d][1]) % 4].append(d)
    while len(depth) < 16:
        for v, d in PARENT.items():
            up = ((v[0] - DIRS[d][0]) % 4, (v[1] - DIRS[d][1]) % 4)
            if up in depth:
                depth[v] = depth[up] + 1
    child = [sum(1 << (4 * v[0] + v[1]) for v in kids if d in kids[v]) for d in range(4)]
    bits = [sum(1 << (4 * v[0] + v[1]) for v in depth if depth[v] >> n & 1) for n in range(3)]
    return child, bits


CHILD, DEPTH = tree_tables()


WORK = tuple((1, b) for b in range(8)) + tuple((0, b) for b in range(4))
UPPER = tuple((0, b) for b in range(4, 8))


def bit(mask, n):
    hit = False
    for i in range(16):
        if mask >> i & 1:
            hit = (n == i) | hit
    return hit


def kernel(x, o, tiles, cols, rows, corner, fac, cm, linv, phi, plo, cthi, ctlo, tchi, tclo, trhi, trlo,
           ld, ldc, ldr, st, colsem, givesem, rowsem, csem, fsem, fq, scol, sgive, srow, sc, fz, fx, fy, fk, sq):
    r = lax.axis_index("row")
    z = lax.axis_index("col")
    px, py, k = r // 8, (r // 2) % 4, r % 2
    partner = (r + 1 - 2 * k, z)
    root = (r == 0) & (z == 0)
    src = r < 2
    extra = (r == 1) & (z == 1)

    def load(a, b, h):
        return pltpu.make_async_copy(x.at[a, :, b, h, :], tiles.at[a, b, :, pl.ds(h * H, H)], ld.at[a, b, h])

    def load_col(b, h):
        return pltpu.make_async_copy(x.at[0, :, b, h, :], cols.at[k, b, :, pl.ds(h * H, H)], ldc.at[b, h])

    def load_row(a, h):
        return pltpu.make_async_copy(x.at[a, :, 0, h, :], rows.at[z, a, :, pl.ds(h * H, H)], ldr.at[a, h])

    @pl.when(z < 2)
    def _():
        for a in range(2):
            for h in range(2):
                load_row(a, h).start()

    @pl.when(src)
    def _():
        for b in range(8):
            for h in range(2):
                load_col(b, h).start()

    for a, b in WORK:
        for h in range(2):
            load(a, b, h).start()

    def store(a, b):
        return pltpu.make_async_copy(tiles.at[a, b], o.at[a, b], st.at[a, b])

    barrier = pltpu.get_barrier_semaphore()

    def greet(dev):
        pl.semaphore_signal(barrier, inc=1, device_id=dev, device_id_type=MESH)

    for d in (1, 3):
        greet((((px + d) % 4) * 8 + py * 2 + k, z))
        greet((px * 8 + ((py + d) % 4) * 2 + k, z))
    greet(partner)
    for d in (1, 7):
        greet((r, (z + d) % 8))

    @pl.when(k == 0)
    def _():
        greet((((px + 2) % 4) * 8 + py * 2, z))
        greet((px * 8 + ((py + 2) % 4) * 2, z))

    @pl.when(r == 0)
    def _():
        for d in (2, 6):
            greet((0, (z + d) % 8))

    @pl.when(extra)
    def _():
        greet((0, 0))

    @pl.when(root)
    def _():
        greet((1, 1))

    @pl.when(z < 2)
    def _():
        for a in range(2):
            for h in range(2):
                load_row(a, h).wait()

    @pl.when(root)
    def _():
        for i in range(2):
            for j in range(i + 1):
                cm[i, j] = rows[0, 0, i * H:(i + 1) * H, j * H:(j + 1) * H]
        chol_inv(cm[0, 0], linv)

    peers = 7 + jnp.where(k == 0, 2, 0) + jnp.where(r == 0, 2, 0) + jnp.where(root | extra, 1, 0)
    pl.semaphore_wait(barrier, peers)

    def send(ref, ss, rs, dev, to=None):
        return pltpu.make_async_remote_copy(
            src_ref=ref, dst_ref=ref if to is None else to, send_sem=ss, recv_sem=rs, device_id=dev, device_id_type=MESH)

    def start(c):
        c.start()

    def wait_send(c):
        c.wait_send()

    def corner_send(i, dev):
        return send(rows.at[i, 0], sc.at[0], csem.at[i], dev, corner.at[i])

    def row_send(p, i, d, zz):
        ref = rows.at[p, i // PER, pl.ds((i % PER) * CH, CH)]
        return send(ref, srow.at[p, d], rowsem.at[p, i], (r, zz))

    row_depth = (jnp.where(z < 3, z, 8 - z),
                 jnp.where(z == 0, 1, jnp.where((z == 7) & (r > 0), 2, z - 1)))
    row_down = ((z == 0) | (z > 3), (z == 1) | ((z == 0) & (r > 0)))
    row_up = (z < 2, (z > 0) & ((z < 6) | ((z == 6) & (r == 0))))
    row_from = (z > 0, z != 1)
    row_first = (jnp.where(r == 0, PER, 0), jnp.where(r < 2, PER, 0))

    def row_spread(p, i, act):
        @pl.when(row_down[p])
        def _():
            act(row_send(p, i, 0, (z + 7) % 8))

        @pl.when(row_up[p])
        def _():
            act(row_send(p, i, 1, (z + 1) % 8))

    def row_step(p, step):
        i = step - row_depth[p] * HOP

        @pl.when((i >= row_first[p]) & (i < NC) & (row_down[p] | row_up[p]))
        def _():
            @pl.when(row_from[p])
            def _():
                row_send(p, i, 0, z).wait_recv()
            row_spread(p, i, start)

    frames, links = [], []
    fx_, fy_ = px, py
    for t in range(4):
        n = fx_ * 4 + fy_
        frames.append((bit(DEPTH[0], n).astype(jnp.int32) + 2 * bit(DEPTH[1], n).astype(jnp.int32)
                       + 4 * bit(DEPTH[2], n).astype(jnp.int32)) * HOP)
        links.append([bit(CHILD[d], n) for d in range(4)])
        fx_, fy_ = fy_, (4 - fx_) % 4

    def col_send(t, i, d, dev):
        ref = cols.at[k, t + 4 * (i // PER), pl.ds((i % PER) * CH, CH)]
        return send(ref, scol.at[t, d], colsem.at[t, i], dev)

    def col_spread(t, i, act):
        for d in range(4):
            dx, dy = DIRS[(d + t) % 4]

            @pl.when(links[t][d])
            def _():
                act(col_send(t, i, d, (((px + dx + 4) % 4) * 8 + ((py + dy + 4) % 4) * 2 + k, z)))

    def give(b):
        return send(cols.at[k, b], sgive.at[b], givesem.at[b], partner)

    def col_step(t, step):
        i = step - frames[t]

        @pl.when((i >= 0) & (i < NC))
        def _():
            @pl.when(jnp.logical_not(src))
            def _():
                col_send(t, i, 0, partner).wait_recv()
            col_spread(t, i, start)

            @pl.when(i % PER == PER - 1)
            def _():
                give(t + 4 * (i // PER)).start()

    def use(b):
        return px >= b - 4

    def fac_send(s, ss, dev):
        ref = fac.at[pl.ds(STAGE[s], STAGE[s + 1] - STAGE[s])]
        return send(ref, ss, fsem.at[s], dev)

    def z_spread(s, act):
        for at, to in ZFAN.items():
            @pl.when((r == 0) & (z == at))
            def _():
                for d in to:
                    act(fac_send(s, fz.at[s, d - 1], (0, d)))

    def xy_spread(s, act):
        @pl.when(r == 0)
        def _():
            for n in range(3):
                act(fac_send(s, fx.at[s, n], (OTHER[n] * 8, z)))

        @pl.when((py == 0) & (k == 0))
        def _():
            for n in range(3):
                act(fac_send(s, fy.at[s, n], (px * 8 + OTHER[n] * 2, z)))

    def k_spread(s, act):
        @pl.when(k == 0)
        def _():
            act(fac_send(s, fk.at[s], partner))

    def quarter(s, t, d, dev):
        ref = fac.at[pl.ds(STAGE[s], STAGE[s + 1] - STAGE[s]), pl.ds(t * 32, 32)]
        return send(ref, sq.at[s, t, d], fq.at[s, t], dev)

    def q_spread(s, t, act):
        for d in range(4):
            dx, dy = DIRS[(d + t) % 4]

            @pl.when(links[t][d] & (k == 0))
            def _():
                act(quarter(s, t, d, (((px + dx + 4) % 4) * 8 + ((py + dy + 4) % 4) * 2, z)))

    def fac_spread(s, act):
        z_spread(s, act)
        if s < QUARTERED:
            for t in range(4):
                q_spread(s, t, act)
        else:
            xy_spread(s, act)
        k_spread(s, act)

    def fac_wait(s):
        fac_send(s, fk.at[s], partner).wait_recv()

    hub = (r == 0) & (z > 0)
    relay = (k == 0) & (py == 0) & (px > 0)
    inner = (k == 0) & (r > 0)
    far = jnp.where((z == 2) | (z == 6) | (z == 0), 0, FAR)
    kids = [ln[0] | ln[1] | ln[2] | ln[3] for ln in links]

    def quarter_wait(s, t):
        quarter(s, t, 0, partner).wait_recv()

    @pl.when((r == 1) & (z == 0))
    def _():
        corner_send(0, (0, 0)).start()

    @pl.when(extra)
    def _():
        corner_send(1, (0, 0)).start()

    @pl.when(src)
    def _():
        for b in range(8):
            for h in range(2):
                load_col(b, h).wait()

    def step_body(step, c):
        for p in range(2):
            row_step(p, step)
        for t in range(4):
            col_step(t, step)
        @pl.when(hub)
        def _():
            for s in range(4):
                @pl.when(step == ZSTEP[s] + far)
                def _():
                    fac_wait(s)
                    z_spread(s, start)
                    if s >= QUARTERED:
                        xy_spread(s, start)
                    k_spread(s, start)

        @pl.when(relay)
        def _():
            for s in range(QUARTERED, 4):
                @pl.when(step == ZSTEP[s] + far + FAR)
                def _():
                    fac_wait(s)
                    xy_spread(s, start)
                    k_spread(s, start)

        if QUARTERED:
            @pl.when((hub | inner) & (step >= QSTEP[0]))
            def _():
                for t in range(4):
                    for s in range(QUARTERED):
                        @pl.when((step == QSTEP[s] + frames[t]) & kids[t])
                        def _():
                            @pl.when(inner)
                            def _():
                                quarter_wait(s, t)
                            q_spread(s, t, start)
        return c

    lax.fori_loop(0, jnp.where(root, NC, STEPS), step_body, 0)

    @pl.when(root)
    def _():
        for i in range(2):
            send(rows.at[0, 0], sc.at[0], csem.at[i], partner, corner.at[i]).wait_recv()
        for i in range(2):
            for j in range(2):
                cm[2 + i, j] = corner[0, i * H:(i + 1) * H, j * H:(j + 1) * H]
            for j in range(i + 1):
                cm[2 + i, 2 + j] = corner[1, i * H:(i + 1) * H, j * H:(j + 1) * H]

        def stage(t, c):
            @pl.when(t > 0)
            def _():
                chol_inv(cm[t, t], linv)
            for s in range(4):
                @pl.when(t == s)
                def _():
                    fac[blk(s, s)] = linv[...]
                    for i in range(s + 1, 4):
                        fac[blk(i, s)] = dot_hi(cm[i, s], linv[...])
                    fac_spread(s, start)
                    for i in range(s + 1, 4):
                        for j in range(s + 1, i + 1):
                            cm[i, j] = cm[i, j] - dot_hi(fac[blk(i, s)], fac[blk(j, s)])
            return c

        lax.fori_loop(0, 4, stage, 0)

    for p in range(2):
        @pl.when(row_from[p] & jnp.logical_not(row_down[p] | row_up[p]))
        def _():
            def body(i, c):
                row_send(p, i, 0, z).wait_recv()
                return c
            lax.fori_loop(row_first[p], NC, body, 0)

    for a, b in UPPER:
        tiles[a, b] = jnp.zeros((NB, NB), F32)
        store(a, b).start()

    @pl.when(inner)
    def _():
        for s in range(QUARTERED):
            for t in range(4):
                @pl.when(jnp.logical_not(kids[t]))
                def _():
                    quarter_wait(s, t)
            k_spread(s, start)

    for b in range(8):
        give(b).wait_recv()

    for a, b in WORK:
        for h in range(2):
            load(a, b, h).wait()

    def lefts(s):
        return split(jnp.concatenate([fac[blk(s, m)] for m in range(s)], axis=1))

    def prepare(s):
        w = (s % 2) * H
        done = slice(0, s * H)
        fl = lefts(s)
        for a in range(2):
            trhi[a], trlo[a] = split(rows[s // 2, a, :, w:w + H] - dot3((phi[a, :, done], plo[a, :, done]), fl, NT))
        for b in range(8):
            tchi[b], tclo[b] = split(cols[s // 2, b, w:w + H, :] - dot3(fl, (cthi[b, done, :], ctlo[b, done, :]), NN))

    def solve(s):
        w = (s % 2) * H
        at = slice(s * H, (s + 1) * H)
        fs = split(fac[blk(s, s)])
        for a in range(2):
            t = (trhi[a], trlo[a]) if s else split(rows[0, a, :, :H])
            t = dot3(t, fs, NT)
            phi[a, :, at], plo[a, :, at] = split(t)

            @pl.when((z == s // 2) & (r + 32 * a >= z))
            def _():
                if w == 0:
                    tiles[a, 0, :, H:] = jnp.zeros((NB, H), F32)
                tiles[a, 0, :, w:w + H] = t
        for b in range(8):
            t = (tchi[b], tclo[b]) if s else split(cols[0, b, :H, :])
            cthi[b, at, :], ctlo[b, at, :] = split(dot3(fs, t, NN))

    ri = lax.broadcasted_iota(jnp.int32, (NB, NB), 0)
    ci = lax.broadcasted_iota(jnp.int32, (NB, NB), 1)

    def update(lo, hi, last):
        at = slice(lo * H, hi * H)
        for a, b in WORK:
            d = dot3((phi[a, :, at], plo[a, :, at]), (cthi[b, at, :], ctlo[b, at, :]), NN)
            if b == 0:
                d = jnp.where(z < 2, 0.0, d)
            d = tiles[a, b] - d
            if last:
                keep = r + 32 * a >= z + 8 * b
                if (a, b) == (0, 0):
                    keep = keep & ((ri >= ci) | (z > 1) | (r != z))
                d = jnp.where(keep, d, 0.0)
            tiles[a, b] = d
            if last:
                store(a, b).start()

    for s in range(4):
        @pl.when((k == 1) | (inner & (s >= QUARTERED) & jnp.logical_not(relay)))
        def _():
            fac_wait(s)
            if s >= QUARTERED:
                k_spread(s, start)
        solve(s)
        if s == 1:
            update(0, 2, False)
        if s < 3:
            prepare(s + 1)
    update(2, 4, True)

    @pl.when((r == 1) & (z == 0))
    def _():
        corner_send(0, (0, 0)).wait_send()

    @pl.when(extra)
    def _():
        corner_send(1, (0, 0)).wait_send()

    for p in range(2):
        for d, on in ((0, row_down[p]), (1, row_up[p])):
            @pl.when(on & (row_first[p] == 0))
            def _():
                send(rows.at[p], srow.at[p, d], rowsem.at[p, 0], partner).wait_send()

            @pl.when(on & (row_first[p] > 0))
            def _():
                send(rows.at[p, 1], srow.at[p, d], rowsem.at[p, 0], partner).wait_send()
    for t in range(4):
        for d in range(4):
            @pl.when(links[t][d])
            def _():
                send(cols.at[k, pl.ds(0, 2)], scol.at[t, d], colsem.at[t, 0], partner).wait_send()
    for b in range(8):
        give(b).wait_send()
    for s in range(4):
        fac_spread(s, wait_send)
    for a, b in WORK + UPPER:
        store(a, b).wait()


def writer(t, o, buf, isem, osem):
    def get(a, b):
        return pltpu.make_async_copy(t.at[a, b], buf.at[a, b], isem.at[a, b])

    def put(a, b, h):
        return pltpu.make_async_copy(buf.at[a, b, :, pl.ds(h * H, H)], o.at[a, :, b, h, :], osem.at[a, b, h])

    which = [(a, b) for a in range(2) for b in range(8)]
    for w in which:
        get(*w).start()
    for w in which:
        get(*w).wait()
        for h in range(2):
            put(*w, h).start()
    for w in which:
        for h in range(2):
            put(*w, h).wait()


def on_device(trailing_in):
    x = trailing_in.reshape(2, NB, 8, 2, H)
    dma = pltpu.SemaphoreType.DMA
    t = pl.pallas_call(
        kernel,
        out_shape=jax.ShapeDtypeStruct((2, 8, NB, NB), F32),
        in_specs=[pl.BlockSpec(memory_space=pl.ANY)],
        out_specs=pl.BlockSpec(memory_space=pl.ANY),
        scratch_shapes=[
            pltpu.VMEM((2, 8, NB, NB), F32),
            pltpu.VMEM((2, 8, NB, NB), F32),
            pltpu.VMEM((2, 2, NB, NB), F32),
            pltpu.VMEM((2, NB, NB), F32),
            pltpu.VMEM((10, H, H), F32),
            pltpu.VMEM((4, 4, H, H), F32),
            pltpu.VMEM((H, H), F32),
            pltpu.VMEM((2, NB, 2 * NB), BF),
            pltpu.VMEM((2, NB, 2 * NB), BF),
            pltpu.VMEM((8, 2 * NB, NB), BF),
            pltpu.VMEM((8, 2 * NB, NB), BF),
            pltpu.VMEM((8, H, NB), BF),
            pltpu.VMEM((8, H, NB), BF),
            pltpu.VMEM((2, NB, H), BF),
            pltpu.VMEM((2, NB, H), BF),
            dma((2, 8, 2)), dma((8, 2)), dma((2, 2)), dma((2, 8)),
            dma((4, NC)), dma((8,)), dma((2, NC)), dma((2,)), dma((4,)), dma((2, 4)),
            dma((4, 4)), dma((8,)), dma((2, 2)), dma((1,)),
            dma((4, 7)), dma((4, 3)), dma((4, 3)), dma((4,)), dma((2, 4, 4)),
        ],
        compiler_params=pltpu.CompilerParams(
            collective_id=0, has_side_effects=True, vmem_limit_bytes=56 << 20
        ),
    )(x)
    out = pl.pallas_call(
        writer,
        out_shape=jax.ShapeDtypeStruct(x.shape, F32),
        in_specs=[pl.BlockSpec(memory_space=pl.ANY)],
        out_specs=pl.BlockSpec(memory_space=pl.ANY),
        scratch_shapes=[pltpu.VMEM((2, 8, NB, NB), F32), dma((2, 8)), dma((2, 8, 2))],
        compiler_params=pltpu.CompilerParams(vmem_limit_bytes=56 << 20),
    )(t)
    return out.reshape(trailing_in.shape)


def solution(mesh):
    spec = P(None, "row", None, None, "col", None)
    return jax.shard_map(on_device, mesh=mesh, in_specs=(spec,), out_specs=spec, check_vma=False)
```

```python
import jax
import jax.numpy as jnp
from jax import lax
from jax.experimental import pallas as pl
from jax.experimental.pallas import tpu as pltpu
from jax.sharding import PartitionSpec as P

NB = 256
H = 128
F32 = jnp.float32
BF = jnp.bfloat16
HI = lax.Precision.HIGHEST
MESH = pl.DeviceIdType.MESH
NT = (((1,), (1,)), ((), ()))
NN = (((1,), (0,)), ((), ()))
STAGE = (0, 4, 7, 9, 10)


def blk(i, k):
    return STAGE[k] + i - k


def lane_splat(x, j):
    return jnp.broadcast_to(x[:, j:j + 1], (8, H))


def row_splat(x, s):
    return jnp.broadcast_to(x[s:s + 1, :], (8, H))


def tree(xs):
    xs = list(xs)
    while len(xs) > 1:
        xs = [xs[i] + xs[i + 1] if i + 1 < len(xs) else xs[i] for i in range(0, len(xs), 2)]
    return xs[0]


def assemble(v, sub):
    b0, b1, b2 = (sub & 1) == 1, (sub & 2) == 2, (sub & 4) == 4
    a = [v[2 * i] if v[2*i] is v[2*i+1] else jnp.where(b0, v[2 * i + 1], v[2 * i]) for i in range(4)]
    b = [a[2 * i] if a[2*i] is a[2*i+1] else jnp.where(b1, a[2 * i + 1], a[2 * i]) for i in range(2)]
    return b[0] if b[0] is b[1] else jnp.where(b2, b[1], b[0])


def chol_inv(a, out_ref, n=16):
    sub = lax.broadcasted_iota(jnp.int32, (8, H), 0)
    lane = lax.broadcasted_iota(jnp.int32, (8, H), 1)
    zero = jnp.zeros((8, H), F32)
    one = jnp.ones((8, H), F32)
    A = [a[8 * g:8 * g + 8, :] for g in range(n)]
    I = [jnp.where(lane == sub + 8 * g, 1.0, 0.0).astype(F32) for g in range(n)]
    c = [lane_splat(A[0], j) for j in range(8)]
    for k in range(n):
        w = 8 * k
        more = k + 1 < n
        if more:
            a1 = [lane_splat(A[k + 1], w + s) for s in range(8)]
            cn = [lane_splat(A[k + 1], w + 8 + j) for j in range(8)]
        D = {(t, j): row_splat(c[j], t) for j in range(8) for t in range(j, 8)}
        rec, rs, l = [], [], {}
        for s in range(8):
            p = D[s, s]
            r = 1.0 / p
            rec.append(r)
            rs.append(lax.rsqrt(p))
            for t in range(s + 1, 8):
                l[t, s] = D[t, s] * r
            for j in range(s + 1, 8):
                for t in range(j, 8):
                    D[t, j] = D[t, j] - l[t, s] * D[j, s]
            if more:
                x = a1[s]
                m = x * r
                for j in range(8):
                    cn[j] = cn[j] - m * row_splat(x, j)
                for t in range(s + 1, 8):
                    a1[t] = a1[t] - x * l[t, s]
        u = {}
        for j in range(8):
            for t in range(j + 1, 8):
                u[t, j] = -tree([l[t, j]] + [l[t, m] * u[m, j] for m in range(j + 1, t)])
        S, T = A[k], I[k]
        ucol = [assemble([zero if t < s else (one if t == s else u[t, s]) for t in range(8)], sub) for s in range(8)]
        T1 = tree([ucol[s] * row_splat(T, s) for s in range(8)])
        out_ref[w:w + 8, :] = assemble(rs, sub) * T1
        if more:
            recv = assemble(rec, sub)
            S1 = tree([ucol[s] * row_splat(S, s) for s in range(8)]) * recv
            T2 = T1 * recv
            vcol = [assemble([u[t, s] if s < t else (one if s == t else zero) for s in range(8)], sub) for t in range(8)]
            Z = tree([vcol[t] * row_splat(S1, t) for t in range(8)])
            ZT = tree([vcol[t] * row_splat(T2, t) for t in range(8)])
            zrow = [row_splat(Z, s) for s in range(8)]
            ztrow = [row_splat(ZT, s) for s in range(8)]
            for g in range(k + 1, n):
                ag = [lane_splat(A[g], w + s) for s in range(8)]
                A[g] = A[g] - tree([ag[s] * zrow[s] for s in range(8)])
                I[g] = I[g] - tree([ag[s] * ztrow[s] for s in range(8)])
            c = cn


def split(a):
    h = a.astype(BF)
    return h, (a - h.astype(F32)).astype(BF)


def dot3(a, b, dims):
    def g(p, q):
        return lax.dot_general(p, q, dims, preferred_element_type=F32)
    return g(a[0], b[0]) + (g(a[0], b[1]) + g(a[1], b[0]))


def dot_nn(a, b):
    return lax.dot_general(a, b, NN, precision=HI, preferred_element_type=F32)


def dot_hi(a, b):
    return lax.dot_general(a, b, NT, precision=HI, preferred_element_type=F32)


CH = 64
NC = 2 * NB // CH
PER = NB // CH
HOP = 3
DIRS = ((1, 0), (0, 1), (-1, 0), (0, -1))
PARENT = {(1, 0): 0, (2, 0): 0, (1, 1): 1, (1, 3): 3, (2, 1): 0, (1, 2): 1, (0, 1): 2, (0, 3): 2,
          (3, 0): 0, (2, 3): 3, (2, 2): 0, (0, 2): 2, (3, 1): 0, (3, 3): 0, (3, 2): 0}
ZSTEP = (8, 10, 13, 16)
FAR = 3
STEPS = max(NC + 5 * HOP, ZSTEP[3] + 2 * FAR + 1)
OTHER = (2, 1, 3)
ZFAN = {0: (2, 6), 2: (4, 3, 1), 6: (5, 7)}


def tree_tables():
    depth = {(0, 0): 0}
    kids = {v: [] for v in list(PARENT) + [(0, 0)]}
    for v, d in PARENT.items():
        kids[(v[0] - DIRS[d][0]) % 4, (v[1] - DIRS[d][1]) % 4].append(d)
    while len(depth) < 16:
        for v, d in PARENT.items():
            up = ((v[0] - DIRS[d][0]) % 4, (v[1] - DIRS[d][1]) % 4)
            if up in depth:
                depth[v] = depth[up] + 1
    child = [sum(1 << (4 * v[0] + v[1]) for v in kids if d in kids[v]) for d in range(4)]
    bits = [sum(1 << (4 * v[0] + v[1]) for v in depth if depth[v] >> n & 1) for n in range(3)]
    return child, bits


CHILD, DEPTH = tree_tables()


WORK = tuple((1, b) for b in range(8)) + tuple((0, b) for b in range(4))
UPPER = tuple((0, b) for b in range(4, 8))


def bit(mask, n):
    hit = False
    for i in range(16):
        if mask >> i & 1:
            hit = (n == i) | hit
    return hit


def kernel(x, o, tiles, cols, rows, corner, fac, cm, linv, phi, plo, cthi, ctlo, tchi, tclo, trhi, trlo,
           ld, ldc, ldr, st, colsem, givesem, rowsem, csem, fsem, scol, sgive, srow, sc, fz, fx, fy, fk):
    r = lax.axis_index("row")
    z = lax.axis_index("col")
    px, py, k = r // 8, (r // 2) % 4, r % 2
    partner = (r + 1 - 2 * k, z)
    root = (r == 0) & (z == 0)
    src = r < 2
    extra = (r == 1) & (z == 1)

    def load(a, b, h):
        return pltpu.make_async_copy(x.at[a, :, b, h, :], tiles.at[a, b, :, pl.ds(h * H, H)], ld.at[a, b, h])

    def load_col(b, h):
        return pltpu.make_async_copy(x.at[0, :, b, h, :], cols.at[k, b, :, pl.ds(h * H, H)], ldc.at[b, h])

    def load_row(a, h):
        return pltpu.make_async_copy(x.at[a, :, 0, h, :], rows.at[z, a, :, pl.ds(h * H, H)], ldr.at[a, h])

    @pl.when(z < 2)
    def _():
        for a in range(2):
            for h in range(2):
                load_row(a, h).start()

    @pl.when(src)
    def _():
        for b in range(8):
            for h in range(2):
                load_col(b, h).start()

    for a, b in WORK:
        for h in range(2):
            load(a, b, h).start()

    def store(a, b):
        return pltpu.make_async_copy(tiles.at[a, b], o.at[a, b], st.at[a, b])

    barrier = pltpu.get_barrier_semaphore()

    def greet(dev):
        pl.semaphore_signal(barrier, inc=1, device_id=dev, device_id_type=MESH)

    for d in (1, 3):
        greet((((px + d) % 4) * 8 + py * 2 + k, z))
        greet((px * 8 + ((py + d) % 4) * 2 + k, z))
    greet(partner)
    for d in (1, 7):
        greet((r, (z + d) % 8))

    @pl.when(k == 0)
    def _():
        greet((((px + 2) % 4) * 8 + py * 2, z))
        greet((px * 8 + ((py + 2) % 4) * 2, z))

    @pl.when(r == 0)
    def _():
        for d in (2, 6):
            greet((0, (z + d) % 8))

    @pl.when(extra)
    def _():
        greet((0, 0))

    @pl.when(root)
    def _():
        greet((1, 1))

    @pl.when(z < 2)
    def _():
        for a in range(2):
            for h in range(2):
                load_row(a, h).wait()

    @pl.when(root)
    def _():
        for i in range(2):
            for j in range(i + 1):
                cm[i, j] = rows[0, 0, i * H:(i + 1) * H, j * H:(j + 1) * H]
        chol_inv(cm[0, 0], linv)

    peers = 7 + jnp.where(k == 0, 2, 0) + jnp.where(r == 0, 2, 0) + jnp.where(root | extra, 1, 0)
    pl.semaphore_wait(barrier, peers)

    def send(ref, ss, rs, dev, to=None):
        return pltpu.make_async_remote_copy(
            src_ref=ref, dst_ref=ref if to is None else to, send_sem=ss, recv_sem=rs, device_id=dev, device_id_type=MESH)

    def start(c):
        c.start()

    def wait_send(c):
        c.wait_send()

    def corner_send(i, dev):
        return send(rows.at[i, 0], sc.at[0], csem.at[i], dev, corner.at[i])

    def row_send(p, i, d, zz):
        ref = rows.at[p, i // PER, pl.ds((i % PER) * CH, CH)]
        return send(ref, srow.at[p, d], rowsem.at[p, i], (r, zz))

    row_depth = (jnp.where(z < 3, z, 8 - z),
                 jnp.where(z == 0, 1, jnp.where((z == 7) & (r > 0), 2, z - 1)))
    row_down = ((z == 0) | (z > 3), (z == 1) | ((z == 0) & (r > 0)))
    row_up = (z < 2, (z > 0) & ((z < 6) | ((z == 6) & (r == 0))))
    row_from = (z > 0, z != 1)
    row_first = (jnp.where(r == 0, PER, 0), jnp.where(r < 2, PER, 0))

    def row_spread(p, i, act):
        @pl.when(row_down[p])
        def _():
            act(row_send(p, i, 0, (z + 7) % 8))

        @pl.when(row_up[p])
        def _():
            act(row_send(p, i, 1, (z + 1) % 8))

    def row_step(p, step):
        i = step - row_depth[p] * HOP

        @pl.when((i >= row_first[p]) & (i < NC) & (row_down[p] | row_up[p]))
        def _():
            @pl.when(row_from[p])
            def _():
                row_send(p, i, 0, z).wait_recv()
            row_spread(p, i, start)

    frames, links = [], []
    fx_, fy_ = px, py
    for t in range(4):
        n = fx_ * 4 + fy_
        frames.append((bit(DEPTH[0], n).astype(jnp.int32) + 2 * bit(DEPTH[1], n).astype(jnp.int32)
                       + 4 * bit(DEPTH[2], n).astype(jnp.int32)) * HOP)
        links.append([bit(CHILD[d], n) for d in range(4)])
        fx_, fy_ = fy_, (4 - fx_) % 4

    def col_send(t, i, d, dev):
        ref = cols.at[k, t + 4 * (i // PER), pl.ds((i % PER) * CH, CH)]
        return send(ref, scol.at[t, d], colsem.at[t, i], dev)

    def col_spread(t, i, act):
        for d in range(4):
            dx, dy = DIRS[(d + t) % 4]

            @pl.when(links[t][d])
            def _():
                act(col_send(t, i, d, (((px + dx + 4) % 4) * 8 + ((py + dy + 4) % 4) * 2 + k, z)))

    def give(b):
        return send(cols.at[k, b], sgive.at[b], givesem.at[b], partner)

    def col_step(t, step):
        i = step - frames[t]

        @pl.when((i >= 0) & (i < NC))
        def _():
            @pl.when(jnp.logical_not(src))
            def _():
                col_send(t, i, 0, partner).wait_recv()
            col_spread(t, i, start)

            @pl.when(i % PER == PER - 1)
            def _():
                give(t + 4 * (i // PER)).start()

    def use(b):
        return px >= b - 4

    def fac_send(j, ss, dev):
        return send(fac.at[j], ss, fsem.at[j], dev)

    def z_spread(js, act):
        for at, to in ZFAN.items():
            @pl.when((r == 0) & (z == at))
            def _():
                for j in js:
                    for d in to:
                        act(fac_send(j, fz.at[j, d - 1], (0, d)))

    def xy_spread(js, act):
        @pl.when(r == 0)
        def _():
            for j in js:
                for n in range(3):
                    act(fac_send(j, fx.at[j, n], (OTHER[n] * 8, z)))

        @pl.when((py == 0) & (k == 0))
        def _():
            for j in js:
                for n in range(3):
                    act(fac_send(j, fy.at[j, n], (px * 8 + OTHER[n] * 2, z)))

    def k_spread(js, act):
        @pl.when(k == 0)
        def _():
            for j in js:
                act(fac_send(j, fk.at[j], partner))

    def fac_spread(js, act):
        z_spread(js, act)
        xy_spread(js, act)
        k_spread(js, act)

    def fac_wait(j):
        fac_send(j, fk.at[j], partner).wait_recv()

    def blocks(s):
        return range(STAGE[s], STAGE[s + 1])

    hub = (r == 0) & (z > 0)
    relay = (k == 0) & (py == 0) & (px > 0)
    inner = (k == 0) & (r > 0)
    far = jnp.where((z == 2) | (z == 6) | (z == 0), 0, FAR)
    @pl.when((r == 1) & (z == 0))
    def _():
        corner_send(0, (0, 0)).start()

    @pl.when(extra)
    def _():
        corner_send(1, (0, 0)).start()

    @pl.when(src)
    def _():
        for b in range(8):
            for h in range(2):
                load_col(b, h).wait()

    def step_body(step, c):
        for p in range(2):
            row_step(p, step)
        for t in range(4):
            col_step(t, step)
        @pl.when(hub)
        def _():
            for s in range(4):
                @pl.when(step == ZSTEP[s] + far)
                def _():
                    for j in blocks(s):
                        fac_wait(j)
                        fac_spread([j], start)

        @pl.when(relay)
        def _():
            for s in range(4):
                @pl.when(step == ZSTEP[s] + far + FAR)
                def _():
                    for j in blocks(s):
                        fac_wait(j)
                        xy_spread([j], start)
                        k_spread([j], start)

        return c

    lax.fori_loop(0, jnp.where(root, NC, STEPS), step_body, 0)

    @pl.when(root)
    def _():
        for i in range(2):
            send(rows.at[0, 0], sc.at[0], csem.at[i], partner, corner.at[i]).wait_recv()
        for i in range(2):
            for j in range(2):
                cm[2 + i, j] = corner[0, i * H:(i + 1) * H, j * H:(j + 1) * H]
            for j in range(i + 1):
                cm[2 + i, 2 + j] = corner[1, i * H:(i + 1) * H, j * H:(j + 1) * H]

        def stage(t, c):
            @pl.when(t > 0)
            def _():
                chol_inv(cm[t, t], linv)
            for s in range(4):
                @pl.when(t == s)
                def _():
                    fac[blk(s, s)] = linv[...]
                    fac_spread([blk(s, s)], start)
                    for i in range(s + 1, 4):
                        fac[blk(i, s)] = dot_hi(cm[i, s], linv[...])
                        fac_spread([blk(i, s)], start)
                    for i in range(s + 1, 4):
                        for j in range(s + 1, i + 1):
                            cm[i, j] = cm[i, j] - dot_hi(fac[blk(i, s)], fac[blk(j, s)])
            return c

        lax.fori_loop(0, 4, stage, 0)

    for p in range(2):
        @pl.when(row_from[p] & jnp.logical_not(row_down[p] | row_up[p]))
        def _():
            def body(i, c):
                row_send(p, i, 0, z).wait_recv()
                return c
            lax.fori_loop(row_first[p], NC, body, 0)

    for b in range(8):
        give(b).wait_recv()

    for a, b in WORK:
        for h in range(2):
            load(a, b, h).wait()

    def inverse(p):
        lo, hi = 2 * p, 2 * p + 1
        a, b = fac[blk(lo, lo)], fac[blk(hi, hi)]
        m = dot_nn(dot_nn(b, fac[blk(hi, lo)]), a)
        top = jnp.concatenate([a, jnp.zeros((H, H), F32)], axis=1)
        return split(jnp.concatenate([top, jnp.concatenate([-m, b], axis=1)], axis=0))

    def prepare():
        left = split(jnp.concatenate([jnp.concatenate([fac[blk(i, m)] for m in range(2)], axis=1) for i in (2, 3)], axis=0))
        for a in range(2):
            trhi[a], trlo[a] = split(rows[1, a] - dot3((phi[a, :, :NB], plo[a, :, :NB]), left, NT))
        for b in range(8):
            tchi[b], tclo[b] = split(cols[1, b] - dot3(left, (cthi[b, :NB, :], ctlo[b, :NB, :]), NN))

    def solve(p):
        at = slice(p * NB, (p + 1) * NB)
        inv = inverse(p)
        for a in range(2):
            t = dot3((trhi[a], trlo[a]) if p else split(rows[0, a]), inv, NT)
            phi[a, :, at], plo[a, :, at] = split(t)

            @pl.when((z == p) & (r + 32 * a >= z))
            def _():
                tiles[a, 0] = t
        for b in range(8):
            t = (tchi[b], tclo[b]) if p else split(cols[0, b])
            cthi[b, at, :], ctlo[b, at, :] = split(dot3(inv, t, NN))

    ri = lax.broadcasted_iota(jnp.int32, (NB, NB), 0)
    ci = lax.broadcasted_iota(jnp.int32, (NB, NB), 1)

    def update(lo, hi, last):
        at = slice(lo * H, hi * H)
        for a, b in WORK:
            d = dot3((phi[a, :, at], plo[a, :, at]), (cthi[b, at, :], ctlo[b, at, :]), NN)
            if b == 0:
                d = jnp.where(z < 2, 0.0, d)
            d = tiles[a, b] - d
            if last:
                keep = r + 32 * a >= z + 8 * b
                if (a, b) == (0, 0):
                    keep = keep & ((ri >= ci) | (z > 1) | (r != z))
                d = jnp.where(keep, d, 0.0)
            tiles[a, b] = d
            if last:
                store(a, b).start()

    def arrive(s):
        @pl.when((k == 1) | (inner & jnp.logical_not(relay)))
        def _():
            for j in blocks(s):
                fac_wait(j)
                k_spread([j], start)

    arrive(0)
    arrive(1)
    solve(0)
    update(0, 2, False)
    prepare()
    arrive(2)
    arrive(3)
    solve(1)
    update(2, 4, True)

    @pl.when((r == 1) & (z == 0))
    def _():
        corner_send(0, (0, 0)).wait_send()

    @pl.when(extra)
    def _():
        corner_send(1, (0, 0)).wait_send()

    for p in range(2):
        for d, on in ((0, row_down[p]), (1, row_up[p])):
            @pl.when(on & (row_first[p] == 0))
            def _():
                send(rows.at[p], srow.at[p, d], rowsem.at[p, 0], partner).wait_send()

            @pl.when(on & (row_first[p] > 0))
            def _():
                send(rows.at[p, 1], srow.at[p, d], rowsem.at[p, 0], partner).wait_send()
    for t in range(4):
        for d in range(4):
            @pl.when(links[t][d])
            def _():
                send(cols.at[k, pl.ds(0, 2)], scol.at[t, d], colsem.at[t, 0], partner).wait_send()
    for b in range(8):
        give(b).wait_send()
    fac_spread(range(10), wait_send)
    for a, b in WORK:
        store(a, b).wait()


def writer(t, o, buf, isem, osem):
    def get(a, b):
        return pltpu.make_async_copy(t.at[a, b], buf.at[a, b], isem.at[a, b])

    def put(a, b, h):
        return pltpu.make_async_copy(buf.at[a, b, :, pl.ds(h * H, H)], o.at[a, :, b, h, :], osem.at[a, b, h])

    for w in WORK:
        get(*w).start()
    for a, b in UPPER:
        buf[a, b] = jnp.zeros((NB, NB), F32)
        for h in range(2):
            put(a, b, h).start()
    for w in WORK:
        get(*w).wait()
        for h in range(2):
            put(*w, h).start()
    for w in WORK + UPPER:
        for h in range(2):
            put(*w, h).wait()


def on_device(trailing_in):
    x = trailing_in.reshape(2, NB, 8, 2, H)
    dma = pltpu.SemaphoreType.DMA
    t = pl.pallas_call(
        kernel,
        out_shape=jax.ShapeDtypeStruct((2, 8, NB, NB), F32),
        in_specs=[pl.BlockSpec(memory_space=pl.ANY)],
        out_specs=pl.BlockSpec(memory_space=pl.ANY),
        scratch_shapes=[
            pltpu.VMEM((2, 8, NB, NB), F32),
            pltpu.VMEM((2, 8, NB, NB), F32),
            pltpu.VMEM((2, 2, NB, NB), F32),
            pltpu.VMEM((2, NB, NB), F32),
            pltpu.VMEM((10, H, H), F32),
            pltpu.VMEM((4, 4, H, H), F32),
            pltpu.VMEM((H, H), F32),
            pltpu.VMEM((2, NB, 2 * NB), BF),
            pltpu.VMEM((2, NB, 2 * NB), BF),
            pltpu.VMEM((8, 2 * NB, NB), BF),
            pltpu.VMEM((8, 2 * NB, NB), BF),
            pltpu.VMEM((8, NB, NB), BF),
            pltpu.VMEM((8, NB, NB), BF),
            pltpu.VMEM((2, NB, NB), BF),
            pltpu.VMEM((2, NB, NB), BF),
            dma((2, 8, 2)), dma((8, 2)), dma((2, 2)), dma((2, 8)),
            dma((4, NC)), dma((8,)), dma((2, NC)), dma((2,)), dma((10,)),
            dma((4, 4)), dma((8,)), dma((2, 2)), dma((1,)),
            dma((10, 7)), dma((10, 3)), dma((10, 3)), dma((10,)),
        ],
        compiler_params=pltpu.CompilerParams(
            collective_id=0, has_side_effects=True, vmem_limit_bytes=56 << 20
        ),
    )(x)
    out = pl.pallas_call(
        writer,
        out_shape=jax.ShapeDtypeStruct(x.shape, F32),
        in_specs=[pl.BlockSpec(memory_space=pl.ANY)],
        out_specs=pl.BlockSpec(memory_space=pl.ANY),
        scratch_shapes=[pltpu.VMEM((2, 8, NB, NB), F32), dma((2, 8)), dma((2, 8, 2))],
        compiler_params=pltpu.CompilerParams(vmem_limit_bytes=56 << 20),
    )(t)
    return out.reshape(trailing_in.shape)


def solution(mesh):
    spec = P(None, "row", None, None, "col", None)
    return jax.shard_map(on_device, mesh=mesh, in_specs=(spec,), out_specs=spec, check_vma=False)
```

```python
import jax
import jax.numpy as jnp
from jax import lax
from jax.experimental import pallas as pl
from jax.experimental.pallas import tpu as pltpu
from jax.sharding import PartitionSpec as P

NB = 256
H = 128
F32 = jnp.float32
BF = jnp.bfloat16
HI = lax.Precision.HIGHEST
MESH = pl.DeviceIdType.MESH
NT = (((1,), (1,)), ((), ()))
NN = (((1,), (0,)), ((), ()))
STAGE = (0, 4, 7, 9, 10)


def blk(i, k):
    return STAGE[k] + i - k


def lane_splat(x, j):
    return jnp.broadcast_to(x[:, j:j + 1], (8, H))


def row_splat(x, s):
    return jnp.broadcast_to(x[s:s + 1, :], (8, H))


def tree(xs):
    xs = list(xs)
    while len(xs) > 1:
        xs = [xs[i] + xs[i + 1] if i + 1 < len(xs) else xs[i] for i in range(0, len(xs), 2)]
    return xs[0]


def assemble(v, sub):
    b0, b1, b2 = (sub & 1) == 1, (sub & 2) == 2, (sub & 4) == 4
    a = [v[2 * i] if v[2*i] is v[2*i+1] else jnp.where(b0, v[2 * i + 1], v[2 * i]) for i in range(4)]
    b = [a[2 * i] if a[2*i] is a[2*i+1] else jnp.where(b1, a[2 * i + 1], a[2 * i]) for i in range(2)]
    return b[0] if b[0] is b[1] else jnp.where(b2, b[1], b[0])


def chol_inv(a, out_ref, n=16):
    sub = lax.broadcasted_iota(jnp.int32, (8, H), 0)
    lane = lax.broadcasted_iota(jnp.int32, (8, H), 1)
    zero = jnp.zeros((8, H), F32)
    one = jnp.ones((8, H), F32)
    A = [a[8 * g:8 * g + 8, :] for g in range(n)]
    I = [jnp.where(lane == sub + 8 * g, 1.0, 0.0).astype(F32) for g in range(n)]
    c = [lane_splat(A[0], j) for j in range(8)]
    for k in range(n):
        w = 8 * k
        more = k + 1 < n
        if more:
            a1 = [lane_splat(A[k + 1], w + s) for s in range(8)]
            cn = [lane_splat(A[k + 1], w + 8 + j) for j in range(8)]
        D = {(t, j): row_splat(c[j], t) for j in range(8) for t in range(j, 8)}
        rec, rs, l = [], [], {}
        for s in range(8):
            p = D[s, s]
            r = 1.0 / p
            rec.append(r)
            rs.append(lax.rsqrt(p))
            for t in range(s + 1, 8):
                l[t, s] = D[t, s] * r
            for j in range(s + 1, 8):
                for t in range(j, 8):
                    D[t, j] = D[t, j] - l[t, s] * D[j, s]
            if more:
                x = a1[s]
                m = x * r
                for j in range(8):
                    cn[j] = cn[j] - m * row_splat(x, j)
                for t in range(s + 1, 8):
                    a1[t] = a1[t] - x * l[t, s]
        u = {}
        for j in range(8):
            for t in range(j + 1, 8):
                u[t, j] = -tree([l[t, j]] + [l[t, m] * u[m, j] for m in range(j + 1, t)])
        S, T = A[k], I[k]
        ucol = [assemble([zero if t < s else (one if t == s else u[t, s]) for t in range(8)], sub) for s in range(8)]
        T1 = tree([ucol[s] * row_splat(T, s) for s in range(8)])
        out_ref[w:w + 8, :] = assemble(rs, sub) * T1
        if more:
            recv = assemble(rec, sub)
            S1 = tree([ucol[s] * row_splat(S, s) for s in range(8)]) * recv
            T2 = T1 * recv
            vcol = [assemble([u[t, s] if s < t else (one if s == t else zero) for s in range(8)], sub) for t in range(8)]
            Z = tree([vcol[t] * row_splat(S1, t) for t in range(8)])
            ZT = tree([vcol[t] * row_splat(T2, t) for t in range(8)])
            zrow = [row_splat(Z, s) for s in range(8)]
            ztrow = [row_splat(ZT, s) for s in range(8)]
            for g in range(k + 1, n):
                ag = [lane_splat(A[g], w + s) for s in range(8)]
                A[g] = A[g] - tree([ag[s] * zrow[s] for s in range(8)])
                I[g] = I[g] - tree([ag[s] * ztrow[s] for s in range(8)])
            c = cn


def split(a):
    h = a.astype(BF)
    return h, (a - h.astype(F32)).astype(BF)


def dot3(a, b, dims):
    def g(p, q):
        return lax.dot_general(p, q, dims, preferred_element_type=F32)
    return g(a[0], b[0]) + (g(a[0], b[1]) + g(a[1], b[0]))


def dot_nn(a, b):
    return lax.dot_general(a, b, NN, precision=HI, preferred_element_type=F32)


def dot_hi(a, b):
    return lax.dot_general(a, b, NT, precision=HI, preferred_element_type=F32)


CH = 64
NC = 2 * NB // CH
PER = NB // CH
HOP = 3
DIRS = ((1, 0), (0, 1), (-1, 0), (0, -1))
PARENT = {(1, 0): 0, (2, 0): 0, (1, 1): 1, (1, 3): 3, (2, 1): 0, (1, 2): 1, (0, 1): 2, (0, 3): 2,
          (3, 0): 0, (2, 3): 3, (2, 2): 0, (0, 2): 2, (3, 1): 0, (3, 3): 0, (3, 2): 0}
ZSTEP = (8, 10, 13, 16)
FAR = 3
STEPS = max(NC + 5 * HOP, ZSTEP[3] + 2 * FAR + 1)
OTHER = (2, 1, 3)
ZFAN = {0: (2, 6), 2: (4, 3, 1), 6: (5, 7)}


def tree_tables():
    depth = {(0, 0): 0}
    kids = {v: [] for v in list(PARENT) + [(0, 0)]}
    for v, d in PARENT.items():
        kids[(v[0] - DIRS[d][0]) % 4, (v[1] - DIRS[d][1]) % 4].append(d)
    while len(depth) < 16:
        for v, d in PARENT.items():
            up = ((v[0] - DIRS[d][0]) % 4, (v[1] - DIRS[d][1]) % 4)
            if up in depth:
                depth[v] = depth[up] + 1
    child = [sum(1 << (4 * v[0] + v[1]) for v in kids if d in kids[v]) for d in range(4)]
    bits = [sum(1 << (4 * v[0] + v[1]) for v in depth if depth[v] >> n & 1) for n in range(3)]
    return child, bits


CHILD, DEPTH = tree_tables()


WORK = tuple((1, b) for b in range(8)) + tuple((0, b) for b in range(4))
UPPER = tuple((0, b) for b in range(4, 8))


def bit(mask, n):
    hit = False
    for i in range(16):
        if mask >> i & 1:
            hit = (n == i) | hit
    return hit


def kernel(x, o, tiles, cols, rows, corner, fac, cm, linv, phi, plo, cthi, ctlo, tchi, tclo, trhi, trlo,
           ld, ldc, ldr, st, colsem, givesem, rowsem, csem, fsem, scol, sgive, srow, sc, fz, fx, fy, fk):
    r = lax.axis_index("row")
    z = lax.axis_index("col")
    px, py, k = r // 8, (r // 2) % 4, r % 2
    partner = (r + 1 - 2 * k, z)
    root = (r == 0) & (z == 0)
    src = r < 2
    extra = (r == 1) & (z == 1)

    def load(a, b, h):
        return pltpu.make_async_copy(x.at[a, :, b, h, :], tiles.at[a, b, :, pl.ds(h * H, H)], ld.at[a, b, h])

    def load_col(b, h):
        return pltpu.make_async_copy(x.at[0, :, b, h, :], cols.at[k, b, :, pl.ds(h * H, H)], ldc.at[b, h])

    def load_row(a, h):
        return pltpu.make_async_copy(x.at[a, :, 0, h, :], rows.at[z, a, :, pl.ds(h * H, H)], ldr.at[a, h])

    @pl.when(z < 2)
    def _():
        for a in range(2):
            for h in range(2):
                load_row(a, h).start()

    @pl.when(src)
    def _():
        for b in range(8):
            for h in range(2):
                load_col(b, h).start()

    for a, b in WORK:
        for h in range(2):
            load(a, b, h).start()

    def store(a, b):
        return pltpu.make_async_copy(tiles.at[a, b], o.at[a, b], st.at[a, b])

    barrier = pltpu.get_barrier_semaphore()

    def greet(dev):
        pl.semaphore_signal(barrier, inc=1, device_id=dev, device_id_type=MESH)

    for d in (1, 3):
        greet((((px + d) % 4) * 8 + py * 2 + k, z))
        greet((px * 8 + ((py + d) % 4) * 2 + k, z))
    greet(partner)
    for d in (1, 7):
        greet((r, (z + d) % 8))

    @pl.when(k == 0)
    def _():
        greet((((px + 2) % 4) * 8 + py * 2, z))
        greet((px * 8 + ((py + 2) % 4) * 2, z))

    @pl.when(r == 0)
    def _():
        for d in (2, 6):
            greet((0, (z + d) % 8))

    @pl.when(extra)
    def _():
        greet((0, 0))

    @pl.when(root)
    def _():
        greet((1, 1))

    @pl.when(z < 2)
    def _():
        for a in range(2):
            for h in range(2):
                load_row(a, h).wait()

    @pl.when(root)
    def _():
        for i in range(2):
            for j in range(i + 1):
                cm[i, j] = rows[0, 0, i * H:(i + 1) * H, j * H:(j + 1) * H]
        chol_inv(cm[0, 0], linv)

    peers = 7 + jnp.where(k == 0, 2, 0) + jnp.where(r == 0, 2, 0) + jnp.where(root | extra, 1, 0)
    pl.semaphore_wait(barrier, peers)

    def send(ref, ss, rs, dev, to=None):
        return pltpu.make_async_remote_copy(
            src_ref=ref, dst_ref=ref if to is None else to, send_sem=ss, recv_sem=rs, device_id=dev, device_id_type=MESH)

    def start(c):
        c.start()

    def wait_send(c):
        c.wait_send()

    def corner_send(i, dev):
        return send(rows.at[i, 0], sc.at[0], csem.at[i], dev, corner.at[i])

    def row_send(p, i, d, zz):
        ref = rows.at[p, i // PER, pl.ds((i % PER) * CH, CH)]
        return send(ref, srow.at[p, d], rowsem.at[p, i], (r, zz))

    row_depth = (jnp.where(z < 3, z, 8 - z),
                 jnp.where(z == 0, 1, jnp.where((z == 7) & (r > 0), 2, z - 1)))
    row_down = ((z == 0) | (z > 3), (z == 1) | ((z == 0) & (r > 0)))
    row_up = (z < 2, (z > 0) & ((z < 6) | ((z == 6) & (r == 0))))
    row_from = (z > 0, z != 1)
    row_first = (jnp.where(r == 0, PER, 0), jnp.where(r < 2, PER, 0))

    def row_spread(p, i, act):
        @pl.when(row_down[p])
        def _():
            act(row_send(p, i, 0, (z + 7) % 8))

        @pl.when(row_up[p])
        def _():
            act(row_send(p, i, 1, (z + 1) % 8))

    def row_step(p, step):
        i = step - row_depth[p] * HOP

        @pl.when((i >= row_first[p]) & (i < NC) & (row_down[p] | row_up[p]))
        def _():
            @pl.when(row_from[p])
            def _():
                row_send(p, i, 0, z).wait_recv()
            row_spread(p, i, start)

    frames, links = [], []
    fx_, fy_ = px, py
    for t in range(4):
        n = fx_ * 4 + fy_
        frames.append((bit(DEPTH[0], n).astype(jnp.int32) + 2 * bit(DEPTH[1], n).astype(jnp.int32)
                       + 4 * bit(DEPTH[2], n).astype(jnp.int32)) * HOP)
        links.append([bit(CHILD[d], n) for d in range(4)])
        fx_, fy_ = fy_, (4 - fx_) % 4

    def col_send(t, i, d, dev):
        ref = cols.at[k, t + 4 * (i // PER), pl.ds((i % PER) * CH, CH)]
        return send(ref, scol.at[t, d], colsem.at[t, i], dev)

    def col_spread(t, i, act):
        for d in range(4):
            dx, dy = DIRS[(d + t) % 4]

            @pl.when(links[t][d])
            def _():
                act(col_send(t, i, d, (((px + dx + 4) % 4) * 8 + ((py + dy + 4) % 4) * 2 + k, z)))

    def give(b):
        return send(cols.at[k, b], sgive.at[b], givesem.at[b], partner)

    def col_step(t, step):
        i = step - frames[t]

        @pl.when((i >= 0) & (i < NC))
        def _():
            @pl.when(jnp.logical_not(src))
            def _():
                col_send(t, i, 0, partner).wait_recv()
            col_spread(t, i, start)

            @pl.when(i % PER == PER - 1)
            def _():
                give(t + 4 * (i // PER)).start()

    def use(b):
        return px >= b - 4

    def fac_send(j, ss, dev):
        return send(fac.at[j], ss, fsem.at[j], dev)

    def z_spread(js, act):
        for at, to in ZFAN.items():
            @pl.when((r == 0) & (z == at))
            def _():
                for j in js:
                    for d in to:
                        act(fac_send(j, fz.at[j, d - 1], (0, d)))

    def xy_spread(js, act):
        @pl.when(r == 0)
        def _():
            for j in js:
                for n in range(3):
                    act(fac_send(j, fx.at[j, n], (OTHER[n] * 8, z)))

        @pl.when((py == 0) & (k == 0))
        def _():
            for j in js:
                for n in range(3):
                    act(fac_send(j, fy.at[j, n], (px * 8 + OTHER[n] * 2, z)))

    def k_spread(js, act):
        @pl.when(k == 0)
        def _():
            for j in js:
                act(fac_send(j, fk.at[j], partner))

    def fac_spread(js, act):
        z_spread(js, act)
        xy_spread(js, act)
        k_spread(js, act)

    def fac_wait(j):
        fac_send(j, fk.at[j], partner).wait_recv()

    def blocks(s):
        return range(STAGE[s], STAGE[s + 1])

    hub = (r == 0) & (z > 0)
    relay = (k == 0) & (py == 0) & (px > 0)
    inner = (k == 0) & (r > 0)
    far = jnp.where((z == 2) | (z == 6) | (z == 0), 0, FAR)
    @pl.when((r == 1) & (z == 0))
    def _():
        corner_send(0, (0, 0)).start()

    @pl.when(extra)
    def _():
        corner_send(1, (0, 0)).start()

    @pl.when(src)
    def _():
        for b in range(8):
            for h in range(2):
                load_col(b, h).wait()

    def step_body(step, c):
        for p in range(2):
            row_step(p, step)
        for t in range(4):
            col_step(t, step)
        @pl.when(hub)
        def _():
            for s in range(4):
                @pl.when(step == ZSTEP[s] + far)
                def _():
                    for j in blocks(s):
                        fac_wait(j)
                        fac_spread([j], start)

        @pl.when(relay)
        def _():
            for s in range(4):
                @pl.when(step == ZSTEP[s] + far + FAR)
                def _():
                    for j in blocks(s):
                        fac_wait(j)
                        xy_spread([j], start)
                        k_spread([j], start)

        return c

    lax.fori_loop(0, jnp.where(root, NC, STEPS), step_body, 0)

    @pl.when(root)
    def _():
        for i in range(2):
            send(rows.at[0, 0], sc.at[0], csem.at[i], partner, corner.at[i]).wait_recv()
        for i in range(2):
            for j in range(2):
                cm[2 + i, j] = corner[0, i * H:(i + 1) * H, j * H:(j + 1) * H]
            for j in range(i + 1):
                cm[2 + i, 2 + j] = corner[1, i * H:(i + 1) * H, j * H:(j + 1) * H]

        def stage(t, c):
            @pl.when(t > 0)
            def _():
                chol_inv(cm[t, t], linv)
            for s in range(4):
                @pl.when(t == s)
                def _():
                    fac[blk(s, s)] = linv[...]
                    fac_spread([blk(s, s)], start)
                    for i in range(s + 1, 4):
                        fac[blk(i, s)] = dot_hi(cm[i, s], linv[...])
                        fac_spread([blk(i, s)], start)
                    for i in range(s + 1, 4):
                        for j in range(s + 1, i + 1):
                            cm[i, j] = cm[i, j] - dot_hi(fac[blk(i, s)], fac[blk(j, s)])
            return c

        lax.fori_loop(0, 4, stage, 0)

    pass_on = inner & jnp.logical_not(relay)

    def arrive(s, who):
        @pl.when(who)
        def _():
            for j in blocks(s):
                fac_wait(j)
                k_spread([j], start)

    for s in range(3):
        arrive(s, (k == 1) | pass_on)

    for p in range(2):
        @pl.when(row_from[p] & jnp.logical_not(row_down[p] | row_up[p]))
        def _():
            def body(i, c):
                row_send(p, i, 0, z).wait_recv()
                return c
            lax.fori_loop(row_first[p], NC, body, 0)

    for b in range(8):
        give(b).wait_recv()

    for a, b in WORK:
        for h in range(2):
            load(a, b, h).wait()

    def inverse(p):
        lo, hi = 2 * p, 2 * p + 1
        a, b = fac[blk(lo, lo)], fac[blk(hi, hi)]
        m = dot_nn(dot_nn(b, fac[blk(hi, lo)]), a)
        top = jnp.concatenate([a, jnp.zeros((H, H), F32)], axis=1)
        return split(jnp.concatenate([top, jnp.concatenate([-m, b], axis=1)], axis=0))

    def prepare():
        left = split(jnp.concatenate([jnp.concatenate([fac[blk(i, m)] for m in range(2)], axis=1) for i in (2, 3)], axis=0))
        for a in range(2):
            trhi[a], trlo[a] = split(rows[1, a] - dot3((phi[a, :, :NB], plo[a, :, :NB]), left, NT))
        for b in range(8):
            tchi[b], tclo[b] = split(cols[1, b] - dot3(left, (cthi[b, :NB, :], ctlo[b, :NB, :]), NN))

    def solve(p):
        at = slice(p * NB, (p + 1) * NB)
        inv = inverse(p)
        for a in range(2):
            t = dot3((trhi[a], trlo[a]) if p else split(rows[0, a]), inv, NT)
            phi[a, :, at], plo[a, :, at] = split(t)

            @pl.when((z == p) & (r + 32 * a >= z))
            def _():
                tiles[a, 0] = t
        for b in range(8):
            t = (tchi[b], tclo[b]) if p else split(cols[0, b])
            cthi[b, at, :], ctlo[b, at, :] = split(dot3(inv, t, NN))

    ri = lax.broadcasted_iota(jnp.int32, (NB, NB), 0)
    ci = lax.broadcasted_iota(jnp.int32, (NB, NB), 1)

    def update(lo, hi, last):
        at = slice(lo * H, hi * H)
        for a, b in WORK:
            d = dot3((phi[a, :, at], plo[a, :, at]), (cthi[b, at, :], ctlo[b, at, :]), NN)
            if b == 0:
                d = jnp.where(z < 2, 0.0, d)
            d = tiles[a, b] - d
            if last:
                keep = r + 32 * a >= z + 8 * b
                if (a, b) == (0, 0):
                    keep = keep & ((ri >= ci) | (z > 1) | (r != z))
                d = jnp.where(keep, d, 0.0)
            tiles[a, b] = d
            if last:
                store(a, b).start()

    solve(0)
    arrive(3, pass_on)
    update(0, 2, False)
    prepare()
    arrive(3, k == 1)
    solve(1)
    update(2, 4, True)

    @pl.when((r == 1) & (z == 0))
    def _():
        corner_send(0, (0, 0)).wait_send()

    @pl.when(extra)
    def _():
        corner_send(1, (0, 0)).wait_send()

    for p in range(2):
        for d, on in ((0, row_down[p]), (1, row_up[p])):
            @pl.when(on & (row_first[p] == 0))
            def _():
                send(rows.at[p], srow.at[p, d], rowsem.at[p, 0], partner).wait_send()

            @pl.when(on & (row_first[p] > 0))
            def _():
                send(rows.at[p, 1], srow.at[p, d], rowsem.at[p, 0], partner).wait_send()
    for t in range(4):
        for d in range(4):
            @pl.when(links[t][d])
            def _():
                send(cols.at[k, pl.ds(0, 2)], scol.at[t, d], colsem.at[t, 0], partner).wait_send()
    for b in range(8):
        give(b).wait_send()
    fac_spread(range(10), wait_send)
    for a, b in WORK:
        store(a, b).wait()


def writer(t, o, buf, isem, osem):
    def get(a, b):
        return pltpu.make_async_copy(t.at[a, b], buf.at[a, b], isem.at[a, b])

    def put(a, b, h):
        return pltpu.make_async_copy(buf.at[a, b, :, pl.ds(h * H, H)], o.at[a, :, b, h, :], osem.at[a, b, h])

    for w in WORK:
        get(*w).start()
    for a, b in UPPER:
        buf[a, b] = jnp.zeros((NB, NB), F32)
        for h in range(2):
            put(a, b, h).start()
    for w in WORK:
        get(*w).wait()
        for h in range(2):
            put(*w, h).start()
    for w in WORK + UPPER:
        for h in range(2):
            put(*w, h).wait()


def on_device(trailing_in):
    x = trailing_in.reshape(2, NB, 8, 2, H)
    dma = pltpu.SemaphoreType.DMA
    t = pl.pallas_call(
        kernel,
        out_shape=jax.ShapeDtypeStruct((2, 8, NB, NB), F32),
        in_specs=[pl.BlockSpec(memory_space=pl.ANY)],
        out_specs=pl.BlockSpec(memory_space=pl.ANY),
        scratch_shapes=[
            pltpu.VMEM((2, 8, NB, NB), F32),
            pltpu.VMEM((2, 8, NB, NB), F32),
            pltpu.VMEM((2, 2, NB, NB), F32),
            pltpu.VMEM((2, NB, NB), F32),
            pltpu.VMEM((10, H, H), F32),
            pltpu.VMEM((4, 4, H, H), F32),
            pltpu.VMEM((H, H), F32),
            pltpu.VMEM((2, NB, 2 * NB), BF),
            pltpu.VMEM((2, NB, 2 * NB), BF),
            pltpu.VMEM((8, 2 * NB, NB), BF),
            pltpu.VMEM((8, 2 * NB, NB), BF),
            pltpu.VMEM((8, NB, NB), BF),
            pltpu.VMEM((8, NB, NB), BF),
            pltpu.VMEM((2, NB, NB), BF),
            pltpu.VMEM((2, NB, NB), BF),
            dma((2, 8, 2)), dma((8, 2)), dma((2, 2)), dma((2, 8)),
            dma((4, NC)), dma((8,)), dma((2, NC)), dma((2,)), dma((10,)),
            dma((4, 4)), dma((8,)), dma((2, 2)), dma((1,)),
            dma((10, 7)), dma((10, 3)), dma((10, 3)), dma((10,)),
        ],
        compiler_params=pltpu.CompilerParams(
            collective_id=0, has_side_effects=True, vmem_limit_bytes=56 << 20
        ),
    )(x)
    out = pl.pallas_call(
        writer,
        out_shape=jax.ShapeDtypeStruct(x.shape, F32),
        in_specs=[pl.BlockSpec(memory_space=pl.ANY)],
        out_specs=pl.BlockSpec(memory_space=pl.ANY),
        scratch_shapes=[pltpu.VMEM((2, 8, NB, NB), F32), dma((2, 8)), dma((2, 8, 2))],
        compiler_params=pltpu.CompilerParams(vmem_limit_bytes=56 << 20),
    )(t)
    return out.reshape(trailing_in.shape)


def solution(mesh):
    spec = P(None, "row", None, None, "col", None)
    return jax.shard_map(on_device, mesh=mesh, in_specs=(spec,), out_specs=spec, check_vma=False)
```
